32 devices in a mesh: row: 8 (over y, x, core), col: 4 (over z).
Axes of the slice: x: 2, y: 2, z: 4, core: 2. Of those that a mesh axis runs over, the one named last changes fastest.
Arguments:
- item_factors: bfloat16 [16, 2048, 256], P('col', 'row'), may hold values from -1 to 1
- tile_counts: int32 [16], P('col'), may hold values from 1024 to 2048, as said below
- observed_tiles: int32 [8, 8], P('row', 'col'), may hold values from 0 to 3, as said below
- mask_words: int32 [1024, 8, 256], P('row', 'col'), may hold values from 0 to 255
- confidence: float32 [1024], P('row'), may hold values from 1 to 40
- previous: bfloat16 [1024, 256], P('row'), may hold values from -6 to 6
Outputs:
- user_factors: float32 [1024, 256], P('row')
The draws below stay inside these ranges and needn't reach their ends.
Inputs may be any that keep to these rules, and one draw needn't show every extreme that they name: `tile_counts`: a tile's slots at and past its count are padding; some tile of the draw has all 2048 slots valid. `observed_tiles`: the 2 entries of one user block and one column group are distinct.
All inputs are finite; a program needn't handle non-finite values.
Results may differ from the reference program's by a relative error of at most 0.0013.
The reference program's roundings to bfloat16 on the way (of `seen` and `weights`) count: a program that leaves them out, or rounds other values in their place, can miss the bound.
Values may be sent and summed in bfloat16 or wider, within the bound.
No kernel may reach another device: no remote copies, remote signals or barrier semaphores. Data moves between devices by JAX's collectives and lax.ppermute only.
A program may use at most 64 MiB of HBM per device.

```python
import math
import jax
import jax.numpy as jnp
from jax import lax

R = 256
TILE = 2048
U_DEV = 128
TILES_COL = 4
OBS = 2
ITERS = 3
USERS = 1024
BLOCKS = 8
GROUPS = 4
TILES = 16
WORDS = 256


def draw_item_factors(key, part):
    key_scale = jax.random.fold_in(key, 11)
    key_base = jax.random.fold_in(key, 12)
    scales = jnp.exp(jax.random.uniform(key_scale, (R,), jnp.float32, jnp.log(0.1), 0.0))
    base = jnp.clip(jax.random.normal(key_base, (TILES, TILE, R), jnp.float32), -4.0, 4.0)
    return (base * scales / jnp.sqrt(jnp.float32(TILES * TILE))).astype(jnp.bfloat16)


def draw_tile_counts(key, part):
    key_count = jax.random.fold_in(key, 21)
    key_full = jax.random.fold_in(key, 22)
    counts = jax.random.randint(key_count, (TILES,), TILE // 2, TILE + 1, jnp.int32)
    chosen = jax.random.randint(key_full, (), 0, TILES, jnp.int32)
    return jnp.where(jnp.arange(TILES, dtype=jnp.int32) == chosen, TILE, counts).astype(jnp.int32)


def draw_observed_tiles(key, part):
    keys = jax.random.split(jax.random.fold_in(key, 31), BLOCKS * GROUPS)
    picks = jax.vmap(lambda key_one: jax.random.permutation(key_one, TILES_COL)[:OBS])(keys)
    return picks.reshape(BLOCKS, GROUPS * OBS).astype(jnp.int32)


def with_ends(values, rng, smallest, top_value):
    shape = values.shape
    index_at = [jax.random.randint(jax.random.fold_in(rng, axis), (), 0, shape[axis]) for axis in range(len(shape))]
    values = values.at[tuple(index_at)].set(smallest)
    longest = shape.index(max(shape))
    index_at[longest] = (index_at[longest] + 1) % shape[longest]
    return values.at[tuple(index_at)].set(top_value)


def block_scale(rng, dims, shards, low, top_value):
    def one(position, parts):
        steps = jax.random.uniform(jax.random.fold_in(jax.random.fold_in(rng, 6), position), (parts,), jnp.float32, low / len(shards), top_value / len(shards))
        return jnp.repeat(jnp.exp(steps), dims[position] // parts).reshape((-1,) + (1,) * (len(dims) - position - 1))

    gain = one(*shards[0])
    for cut in shards[1:]:
        gain = gain * one(*cut)
    return gain


def bell_draw(own_key, dims, width, most, shards=(), kind=jnp.bfloat16):
    values = width * jax.random.normal(own_key, dims, jnp.float32)
    if shards:
        values = values * block_scale(own_key, dims, shards, -0.22, 0.18)
    return jnp.clip(values, -most, most).astype(kind)


def setup_inputs(seed: int = 0) -> dict:
    streams_of = jax.random.split(jax.random.key(seed), 7)
    return {
        "item_factors": draw_item_factors(jax.random.fold_in(streams_of[6], 71), 0),
        "tile_counts": draw_tile_counts(jax.random.fold_in(streams_of[6], 71), 0),
        "observed_tiles": draw_observed_tiles(jax.random.fold_in(streams_of[6], 71), 0),
        "mask_words": with_ends(jax.random.randint(streams_of[3], (USERS, GROUPS * OBS, WORDS), 0, 256), jax.random.fold_in(streams_of[3], 1), 0, 255).astype(jnp.int32),
        "confidence": jnp.clip(jnp.exp(math.log(40.0) - 3.6888795 * jax.random.uniform(streams_of[4], (USERS,), jnp.float32) ** block_scale(streams_of[4], (USERS,), ((0, 8),), -0.2, 0.2)), 1.0, 40.0),
        "previous": bell_draw(streams_of[5], (USERS, R), 1.0, 6.0, ((0, 8),)),
    }


ridge_weight = 0.1


def unpack_bits(words):
    shifts = jnp.arange(8, dtype=jnp.int32)
    bits = jnp.right_shift(words[..., None], shifts) & 1
    return bits.reshape(words.shape[:-1] + (words.shape[-1] * 8,))


def reference(item_factors, tile_counts, observed_tiles, mask_words, confidence, previous):
    slot_index = jnp.arange(TILE, dtype=jnp.int32)

    def add_gram(total, inputs):
        tile_rows, count_now = inputs
        masked = jnp.where((slot_index < count_now)[:, None], tile_rows, jnp.zeros_like(tile_rows))
        return total + jnp.dot(masked.T, masked, preferred_element_type=jnp.float32), None

    gram, _ = lax.scan(add_gram, jnp.zeros((R, R), jnp.float32), (item_factors, tile_counts))
    slots = GROUPS * OBS

    def solve_block(inputs):
        prev_rows, alpha, words, observed = inputs
        tile_ids = ((jnp.arange(slots, dtype=jnp.int32) // OBS) * TILES_COL + observed).astype(jnp.int32)
        tiles = item_factors[tile_ids]
        valid = (slot_index[None, :] < tile_counts[tile_ids][:, None]).astype(jnp.int32)
        seen = (unpack_bits(words) * valid[None]).astype(jnp.bfloat16)
        seen = jnp.transpose(seen, (1, 0, 2))

        def rhs_add(total, pair):
            return total + jnp.dot(pair[1], pair[0], preferred_element_type=jnp.float32), None

        rhs_sum, _ = lax.scan(rhs_add, jnp.zeros((U_DEV, R), jnp.float32), (tiles, seen))
        rhs = (1.0 + alpha)[:, None] * rhs_sum

        def apply_op(vector):
            rounded = vector.astype(jnp.bfloat16)

            def term_add(total, pair):
                tile_rows, seen_now = pair
                scores = jnp.dot(rounded, tile_rows.T, preferred_element_type=jnp.float32)
                weights = (alpha[:, None] * seen_now.astype(jnp.float32) * scores).astype(jnp.bfloat16)
                return total + jnp.dot(weights, tile_rows, preferred_element_type=jnp.float32), None

            summed, _ = lax.scan(term_add, jnp.zeros((U_DEV, R), jnp.float32), (tiles, seen))
            return jnp.dot(vector, gram, precision=lax.Precision.HIGHEST) + ridge_weight * vector + summed

        solution = prev_rows.astype(jnp.float32)
        residual = rhs - apply_op(solution)
        direction = residual
        norm_now = jnp.sum(residual * residual, axis=1)
        for iteration in range(ITERS):
            image = apply_op(direction)
            step_size = norm_now / jnp.sum(direction * image, axis=1)
            solution = solution + step_size[:, None] * direction
            residual = residual - step_size[:, None] * image
            norm_next = jnp.sum(residual * residual, axis=1)
            direction = residual + (norm_next / norm_now)[:, None] * direction
            norm_now = norm_next
        return solution

    result = lax.map(solve_block, (previous.reshape(BLOCKS, U_DEV, R), confidence.reshape(BLOCKS, U_DEV),
                                   mask_words.reshape(BLOCKS, U_DEV, slots, WORDS), observed_tiles))
    return result.reshape(USERS, R)
```

```python
import functools

import jax
import jax.numpy as jnp
from jax import lax
from jax.experimental import pallas as pl
from jax.experimental.pallas import tpu as pltpu
from jax.sharding import PartitionSpec as P

ITERS = 3
BLOCK = 256
PAD = 16
ridge_weight = 0.1

SMEM = pl.BlockSpec(memory_space=pltpu.SMEM)
VMEM = pl.BlockSpec(memory_space=pltpu.VMEM)
F32 = jnp.float32
BF16 = jnp.bfloat16


def call(body, outs, args, n_smem, flops, name):
    return pl.pallas_call(
        body,
        out_shape=[pltpu.VMEM(o.shape, o.dtype) for o in outs],
        in_specs=[SMEM] * n_smem + [VMEM] * (len(args) - n_smem),
        out_specs=[VMEM] * len(outs),
        compiler_params=pltpu.CompilerParams(vmem_limit_bytes=24 * 1024 * 1024),
        cost_estimate=pl.CostEstimate(flops=flops, bytes_accessed=1 << 20, transcendentals=0),
        name=name,
    )(*args)


def column_of(row_values, lanes):
    return jnp.broadcast_to(row_values, (lanes, row_values.shape[1])).T


def row_of(column, rows):
    return jnp.broadcast_to(column, (column.shape[0], 128)).T[:rows]


def pack(values, out_ref):
    users, rank = values.shape
    top = jnp.max(jnp.abs(values), axis=1, keepdims=True)
    power = jnp.ceil(jnp.log2(jnp.maximum(top, 1e-30)))
    scaled = jnp.clip(jnp.round(values * jnp.exp2(15.0 - power)), -32767.0, 32767.0)
    out_ref[:users, :] = scaled.astype(jnp.int32).astype(jnp.int16)
    exponents = row_of(power, PAD).astype(jnp.int32).astype(jnp.int16)
    for at in range(0, rank, users):
        out_ref[users:, at : at + users] = exponents


def unpack(ref):
    users = ref.shape[0] - PAD
    rank = ref.shape[1]
    exponents = ref[users:, :users].astype(jnp.int32).astype(F32)[:1]
    scale = jnp.exp2(column_of(exponents, 128) - 15.0)
    whole = ref[:users, :].astype(jnp.int32).astype(F32)
    return jnp.concatenate([whole[:, at : at + 128] * scale for at in range(0, rank, 128)], axis=1)


def tree_sum(parts):
    while len(parts) > 1:
        parts = [parts[i] + parts[i + 1] for i in range(0, len(parts), 2)]
    return parts[0]


def masks_kernel(pieces, rows, me_ref, picks_ref, counts_ref, words_ref, conf_ref, out_ref):
    me = me_ref[0]
    obs, _, width = words_ref.shape
    lane = lax.broadcasted_iota(jnp.int32, (1, BLOCK), 1)
    word_index = lax.broadcasted_iota(jnp.int32, (width, BLOCK), 0)
    for at in range(0, out_ref.shape[2], BLOCK):
        slot = jnp.zeros((1, BLOCK), jnp.int32)
        for place, shard, offset, length in pieces:
            if at <= place < at + BLOCK:
                start = (me ^ shard) * rows + offset - (place - at)
                slot = jnp.where(lane >= place - at, lane + start, slot)
        spread = (word_index == jnp.right_shift(slot, 3)).astype(BF16)
        for p in range(obs):
            count = counts_ref[picks_ref[p]]
            word = jnp.dot(words_ref[p], spread, preferred_element_type=F32).astype(jnp.int32)
            bits = jnp.right_shift(word, slot & 7) & 1
            bits = jnp.where(slot < count, bits, 0).astype(F32)
            out_ref[p, :, at : at + BLOCK] = bits * conf_ref[...]


def gather_kernel(pieces, rows, place, first, last, *refs):
    me_ref, picks_ref, counts_ref, alpha_ref, conf_ref, prev_ref = refs[:6]
    at = 6
    shards = refs[at : at + len(pieces)]
    at += len(pieces)
    if not first:
        sums_in, gram_in = refs[at : at + 2]
        at += 2
    if last:
        picked_ref, gram_ref, msg_ref = refs[at:]
    else:
        picked_ref, gram_ref, sums_ref = refs[at:]
    me = me_ref[0]
    users, rank = prev_ref.shape
    obs = alpha_ref.shape[0]
    tiles = shards[0].shape[0]
    for p in range(obs):
        tile = picks_ref[p]
        for (spot, _, _, length), ref in zip(pieces, shards):
            picked_ref[p, spot - place : spot - place + length, :] = ref[tile]
    gram = jnp.zeros((rank, rank), F32) if first else gram_in[...]
    for (_, shard, offset, length), ref in zip(pieces, shards):
        slot = lax.broadcasted_iota(jnp.int32, (length, rank), 0) + ((me ^ shard) * rows + offset)
        for t in range(tiles):
            tile_rows = ref[t]
            masked = jnp.where(slot < counts_ref[t], tile_rows, jnp.zeros_like(tile_rows))
            gram = gram + lax.dot_general(
                masked, tile_rows, (((0,), (0,)), ((), ())), preferred_element_type=F32
            )
    gram_ref[...] = gram
    prev = prev_ref[...]
    rhs = jnp.zeros((users, rank), F32) if first else sums_in[0]
    image = jnp.zeros((users, rank), F32) if first else sums_in[1]
    for p in range(obs):
        for start in range(0, picked_ref.shape[1], BLOCK):
            items = picked_ref[p, start : start + BLOCK, :]
            alpha = alpha_ref[p, :, place + start : place + start + BLOCK]
            scores = lax.dot_general(
                prev, items, (((1,), (1,)), ((), ())), preferred_element_type=F32
            )
            weights = (alpha * scores).astype(BF16)
            seen = jnp.where(alpha > 0.0, 1.0, 0.0).astype(BF16)
            rhs = rhs + jnp.dot(seen, items, preferred_element_type=F32)
            image = image + jnp.dot(weights, items, preferred_element_type=F32)
    if last:
        image = image + jnp.dot(prev.astype(F32), gram, precision=lax.Precision.HIGHEST)
        pack((1.0 + conf_ref[...]) * rhs - image, msg_ref)
    else:
        sums_ref[0] = rhs
        sums_ref[1] = image


def round_kernel(step_index, n_msgs, spots, *refs):
    msgs = refs[:n_msgs]
    refs = refs[n_msgs:]
    n_in = 2 if step_index == 0 else 4
    prev_ref, alpha_ref, gram_ref = refs[:3]
    refs = refs[3:]
    picked = refs[: len(spots)]
    refs = refs[len(spots) :]
    summed = tree_sum([unpack(m) for m in msgs])
    if step_index == 0:
        (r_ref, msg_ref) = refs
        residual = summed - ridge_weight * prev_ref[...].astype(F32)
        direction = residual
        r_ref[...] = residual
    else:
        n_state = 1 if step_index == 1 else 3
        state = refs[:n_state]
        refs = refs[n_state:]
        if step_index == 1:
            residual = direction = state[0][...]
            solution = prev_ref[...].astype(F32)
        else:
            residual, direction, solution = (s[...] for s in state)
        image = summed + ridge_weight * direction
        norm_now = jnp.sum(residual * residual, axis=1, keepdims=True)
        step_size = norm_now / jnp.sum(direction * image, axis=1, keepdims=True)
        solution = solution + step_size * direction
        residual = residual - step_size * image
        norm_next = jnp.sum(residual * residual, axis=1, keepdims=True)
        direction = residual + (norm_next / norm_now) * direction
        if step_index < ITERS - 1:
            r_ref, d_ref, x_ref, msg_ref = refs
            r_ref[...] = residual
        else:
            n_ref, d_ref, x_ref, msg_ref = refs
            n_ref[...] = jnp.broadcast_to(norm_next, n_ref.shape)
        d_ref[...] = direction
        x_ref[...] = solution
    last = step_index == ITERS - 1
    rounded = direction.astype(BF16)
    image = jnp.dot(direction, gram_ref[...], precision=lax.Precision.HIGHEST)
    if last:
        total = jnp.sum(image * direction, axis=1, keepdims=True)
        squares = jnp.zeros((direction.shape[0], BLOCK), F32)
    for (place, size), ref in zip(spots, picked):
        for p in range(alpha_ref.shape[0]):
            for start in range(0, size, BLOCK):
                items = ref[p, start : start + BLOCK, :]
                alpha = alpha_ref[p, :, place + start : place + start + BLOCK]
                scores = lax.dot_general(
                    rounded, items, (((1,), (1,)), ((), ())), preferred_element_type=F32
                )
                weights = (alpha * scores).astype(BF16)
                if last:
                    squares = squares + weights.astype(F32) * scores
                else:
                    image = image + jnp.dot(weights, items, preferred_element_type=F32)
    if last:
        total = total + jnp.sum(squares, axis=1, keepdims=True)
        msg_ref[...] = row_of(total, msg_ref.shape[0])
    else:
        pack(image, msg_ref)


def final_kernel(n_msgs, *refs):
    msgs = refs[:n_msgs]
    n_ref, d_ref, x_ref, out_ref = refs[n_msgs:]
    direction = d_ref[...]
    total = column_of(tree_sum([m[...] for m in msgs])[:1], 128)
    squares = jnp.sum(direction * direction, axis=1, keepdims=True)
    step_size = n_ref[...] / (total + ridge_weight * squares)
    for at in range(0, direction.shape[1], 128):
        out_ref[:, at : at + 128] = x_ref[:, at : at + 128] + step_size * direction[:, at : at + 128]


def shifted(array, axis, size, bits):
    return lax.ppermute(array, axis, [(i, i ^ bits) for i in range(size)])


def gather_plan(own, size):
    send = functools.partial(shifted, axis="row", size=size)
    held = {0: own}
    bit = 8
    while bit < size:
        held.update({s ^ bit: send(a, bits=bit) for s, a in held.items()})
        bit *= 2
    if size < 8:
        bit = 1
        while bit < size:
            held.update({s ^ bit: send(a, bits=bit) for s, a in held.items()})
            bit *= 2
        return [[(s, 0, a) for s, a in held.items()]]
    stages = [[], [], []]
    half = own.shape[1] // 2
    for s, a in held.items():
        x, y = send(a, bits=2), send(a, bits=4)
        upper, lower = send(x[:, :half], bits=4), send(y[:, half:], bits=2)
        stages[0] += [(s, 0, a), (s ^ 1, 0, send(a, bits=1))]
        stages[1] += [(s ^ 2, 0, x), (s ^ 3, 0, send(x, bits=1)), (s ^ 4, 0, y), (s ^ 5, 0, send(y, bits=1))]
        stages[2] += [(s ^ 6, 0, upper), (s ^ 7, 0, send(upper, bits=1))]
        stages[2] += [(s ^ 6, half, lower), (s ^ 7, half, send(lower, bits=1))]
    return stages


def local(mesh, item_factors, tile_counts, observed_tiles, mask_words, confidence, previous):
    n_row, n_col = mesh.shape["row"], mesh.shape["col"]
    tiles, rows, rank = item_factors.shape
    users, obs, width = mask_words.shape
    slots = rows * n_row
    me = lax.axis_index("row").astype(jnp.int32).reshape(1)
    picks = observed_tiles[0]
    conf = confidence[:, None]
    words = jnp.transpose(mask_words, (1, 0, 2)).astype(BF16)
    shape = jax.ShapeDtypeStruct

    stages, pieces, place = [], [], 0
    for stage in gather_plan(item_factors, n_row):
        here, start = [], place
        for shard, offset, array in stage:
            here.append((place, shard, offset, array.shape[1]))
            place += array.shape[1]
        stages.append((start, here, [array for _, _, array in stage]))
        pieces += here

    (alpha,) = call(
        functools.partial(masks_kernel, pieces, rows),
        [shape((obs, users, slots), F32)],
        (me, picks, tile_counts, words, conf),
        3,
        2 * obs * users * slots * width,
        "masks",
    )

    message = shape((users + PAD, rank), jnp.int16)
    sums = shape((2, users, rank), F32)
    gram_shape = shape((rank, rank), F32)
    spots, picked, carry = [], [], []
    for index, (start, here, arrays) in enumerate(stages):
        first, last = index == 0, index == len(stages) - 1
        size = sum(length for _, _, _, length in here)
        kept, gram, carried = call(
            functools.partial(gather_kernel, here, rows, start, first, last),
            [shape((obs, size, rank), BF16), gram_shape, message if last else sums],
            (me, picks, tile_counts, alpha, conf, previous, *arrays, *carry),
            3,
            2 * size * rank * (tiles * rank + 3 * obs * users),
            f"stage{index}",
        )
        carry = [carried, gram]
        spots.append((start, size))
        picked.append(kept)
    msg, gram = carry

    def to_all(own):
        return [own] + [shifted(own, "col", n_col, bits) for bits in range(1, n_col)]

    vec = shape((users, rank), F32)
    state = []
    for index in range(ITERS):
        last = index == ITERS - 1
        msgs = to_all(msg)
        outs = [vec] if index == 0 else [vec, vec, vec]
        if last:
            outs = [shape((users, 128), F32), vec, vec]
        outs.append(shape((8, users), F32) if last else message)
        *state, msg = call(
            functools.partial(round_kernel, index, n_col, spots),
            outs,
            (*msgs, previous, alpha, gram, *picked, *state),
            0,
            4 * obs * users * slots * rank,
            f"round{index}",
        )
    msgs = to_all(msg)
    (out,) = pl.pallas_call(
        functools.partial(final_kernel, n_col),
        out_shape=[vec],
        in_specs=[VMEM] * (n_col + 3),
        out_specs=[VMEM],
        name="final",
    )(*msgs, *state)
    return out


def solution(mesh):
    return jax.shard_map(
        functools.partial(local, mesh),
        mesh=mesh,
        in_specs=(
            P("col", "row", None),
            P("col"),
            P("row", "col"),
            P("row", "col", None),
            P("row"),
            P("row", None),
        ),
        out_specs=P("row", None),
        check_vma=False,
    )
```

```python
import functools

import jax
import jax.numpy as jnp
from jax import lax
from jax.experimental import pallas as pl
from jax.experimental.pallas import tpu as pltpu
from jax.sharding import PartitionSpec as P

ITERS = 3
BLOCK = 256
ridge_weight = 0.1

SMEM = pl.BlockSpec(memory_space=pltpu.SMEM)
VMEM = pl.BlockSpec(memory_space=pltpu.VMEM)
F32 = jnp.float32
BF16 = jnp.bfloat16


def call(body, outs, args, n_smem, flops, name):
    return pl.pallas_call(
        body,
        out_shape=[pltpu.VMEM(o.shape, o.dtype) for o in outs],
        in_specs=[SMEM] * n_smem + [VMEM] * (len(args) - n_smem),
        out_specs=[VMEM] * len(outs),
        compiler_params=pltpu.CompilerParams(vmem_limit_bytes=24 * 1024 * 1024),
        cost_estimate=pl.CostEstimate(flops=flops, bytes_accessed=1 << 20, transcendentals=0),
        name=name,
    )(*args)


def column_of(row_values, lanes):
    return jnp.broadcast_to(row_values, (lanes, row_values.shape[1])).T


def row_of(column, rows):
    return jnp.broadcast_to(column, (column.shape[0], 128)).T[:rows]


def low_lanes(users):
    lane = lax.broadcasted_iota(jnp.int32, (users, 128), 1)
    return lane, lane < 8


def pack(values, out_ref):
    users, rank = values.shape
    top = jnp.max(jnp.abs(values), axis=1, keepdims=True)
    power = jnp.clip(jnp.ceil(jnp.log2(jnp.maximum(top, 1e-30))), -100.0, 127.0)
    scaled = jnp.round(values * jnp.exp2(15.0 - power))
    scaled = jnp.clip(scaled, -32767.0, 32767.0).astype(jnp.int32)
    lane, low = low_lanes(users)
    bit = jnp.right_shift(jnp.broadcast_to((power + 128.0).astype(jnp.int32), lane.shape), lane & 7) & 1
    head = scaled[:, :128]
    out_ref[:, :128] = jnp.where(low, (head & -2) | bit, head).astype(jnp.int16)
    out_ref[:, 128:] = scaled[:, 128:].astype(jnp.int16)


def unpack(ref):
    users = ref.shape[0]
    whole = ref[...].astype(jnp.int32)
    head = whole[:, :128]
    lane, low = low_lanes(users)
    bit = jnp.where(low, head & 1, 0)
    power = jnp.sum(jnp.left_shift(bit, lane & 7).astype(F32), axis=1, keepdims=True) - 128.0
    whole = jnp.concatenate([head - bit, whole[:, 128:]], axis=1)
    return whole.astype(F32) * jnp.exp2(power - 15.0)


def tree_sum(parts):
    while len(parts) > 1:
        parts = [parts[i] + parts[i + 1] for i in range(0, len(parts), 2)]
    return parts[0]


def shard_index(me, shards):
    even, odd = shards
    return me ^ (even + (me & 1) * (odd - even))


def masks_kernel(stages, rows, me_ref, picks_ref, counts_ref, words_ref, conf_ref, *out_refs):
    me = me_ref[0]
    obs, _, width = words_ref.shape
    lane = lax.broadcasted_iota(jnp.int32, (1, BLOCK), 1)
    word_index = lax.broadcasted_iota(jnp.int32, (width, BLOCK), 0)
    for pieces, out_ref in zip(stages, out_refs):
        for at in range(0, out_ref.shape[2], BLOCK):
            slot = jnp.zeros((1, BLOCK), jnp.int32)
            for spot, pair, offset, _ in pieces:
                if at <= spot < at + BLOCK:
                    start = shard_index(me, pair) * rows + offset - (spot - at)
                    slot = jnp.where(lane >= spot - at, lane + start, slot)
            spread = (word_index == jnp.right_shift(slot, 3)).astype(BF16)
            for p in range(obs):
                count = counts_ref[picks_ref[p]]
                word = jnp.dot(words_ref[p], spread, preferred_element_type=F32).astype(jnp.int32)
                bits = jnp.right_shift(word, slot & 7) & 1
                bits = jnp.where(slot < count, bits, 0).astype(F32)
                out_ref[p, :, at : at + BLOCK] = bits * conf_ref[...]


def gather_kernel(pieces, rows, first, last, *refs):
    me_ref, picks_ref, counts_ref, alpha_ref, conf_ref, prev_ref = refs[:6]
    at = 6
    arrays = refs[at : at + len(pieces)]
    at += len(pieces)
    if not first:
        gram_in, sums_in = refs[at : at + 2]
        at += 2
    picked_ref, turned_ref = refs[at : at + 2]
    at += 2
    if last:
        high_ref, low_ref, msg_ref = refs[at:]
    else:
        gram_ref, sums_ref = refs[at:]
    me = me_ref[0]
    users, rank = prev_ref.shape
    obs = alpha_ref.shape[0]
    tiles = arrays[0].shape[0]
    for p in range(obs):
        tile = picks_ref[p]
        for (spot, _, _, length), ref in zip(pieces, arrays):
            picked_ref[p, spot : spot + length, :] = ref[tile]
    gram = jnp.zeros((rank, rank), F32) if first else gram_in[...]
    for (_, pair, offset, length), ref in zip(pieces, arrays):
        slot = lax.broadcasted_iota(jnp.int32, (length, rank), 0)
        slot = slot + (shard_index(me, pair) * rows + offset)
        for t in range(tiles):
            tile_rows = ref[t]
            masked = jnp.where(slot < counts_ref[t], tile_rows, jnp.zeros_like(tile_rows))
            gram = gram + lax.dot_general(
                masked, tile_rows, (((0,), (0,)), ((), ())), preferred_element_type=F32
            )
    if last:
        high = gram.astype(BF16)
        low = (gram - high.astype(F32)).astype(BF16)
        high_ref[...] = high
        low_ref[...] = low
    else:
        gram_ref[...] = gram
    prev = prev_ref[...]
    rhs = jnp.zeros((users, rank), F32) if first else sums_in[0]
    image = jnp.zeros((users, rank), F32) if first else sums_in[1]
    for p in range(obs):
        for start in range(0, picked_ref.shape[1], BLOCK):
            items = picked_ref[p, start : start + BLOCK, :]
            turned = items.T
            turned_ref[p, :, start : start + BLOCK] = turned
            alpha = alpha_ref[p, :, start : start + BLOCK]
            scores = jnp.dot(prev, turned, preferred_element_type=F32)
            weights = (alpha * scores).astype(BF16)
            seen = jnp.where(alpha > 0.0, 1.0, 0.0).astype(BF16)
            rhs = rhs + jnp.dot(seen, items, preferred_element_type=F32)
            image = image + jnp.dot(weights, items, preferred_element_type=F32)
    if last:
        image = image + jnp.dot(prev, high, preferred_element_type=F32)
        image = image + jnp.dot(prev, low, preferred_element_type=F32)
        pack((1.0 + conf_ref[...]) * rhs - image, msg_ref)
    else:
        sums_ref[0] = rhs
        sums_ref[1] = image


def round_kernel(step_index, n_msgs, n_stages, *refs):
    msgs = refs[:n_msgs]
    refs = refs[n_msgs:]
    prev_ref, high_ref, low_ref = refs[:3]
    alphas, picked, turned = (refs[3 + n * n_stages : 3 + (n + 1) * n_stages] for n in range(3))
    refs = refs[3 + 3 * n_stages :]
    summed = tree_sum([unpack(m) for m in msgs])
    if step_index == 0:
        (r_ref, msg_ref) = refs
        residual = summed - ridge_weight * prev_ref[...].astype(F32)
        direction = residual
        r_ref[...] = residual
    else:
        n_state = 1 if step_index == 1 else 3
        state = refs[:n_state]
        refs = refs[n_state:]
        if step_index == 1:
            residual = direction = state[0][...]
            solution = prev_ref[...].astype(F32)
        else:
            residual, direction, solution = (s[...] for s in state)
        image = summed + ridge_weight * direction
        norm_now = jnp.sum(residual * residual, axis=1, keepdims=True)
        step_size = norm_now / jnp.sum(direction * image, axis=1, keepdims=True)
        solution = solution + step_size * direction
        residual = residual - step_size * image
        norm_next = jnp.sum(residual * residual, axis=1, keepdims=True)
        direction = residual + (norm_next / norm_now) * direction
        if step_index < ITERS - 1:
            r_ref, d_ref, x_ref, msg_ref = refs
            r_ref[...] = residual
        else:
            n_ref, d_ref, x_ref, msg_ref = refs
            n_ref[...] = jnp.broadcast_to(norm_next, n_ref.shape)
        d_ref[...] = direction
        x_ref[...] = solution
    last = step_index == ITERS - 1
    rounded = direction.astype(BF16)
    users = direction.shape[0]
    both = jnp.concatenate([rounded, (direction - rounded.astype(F32)).astype(BF16)], axis=0)
    both = jnp.dot(both, high_ref[...], preferred_element_type=F32)
    image = both[:users] + both[users:] + jnp.dot(rounded, low_ref[...], preferred_element_type=F32)
    if last:
        total = jnp.sum(image * direction, axis=1, keepdims=True)
        squares = jnp.zeros((direction.shape[0], BLOCK), F32)
    for alpha_ref, ref, turned_ref in zip(alphas, picked, turned):
        for p in range(ref.shape[0]):
            for start in range(0, ref.shape[1], BLOCK):
                items = ref[p, start : start + BLOCK, :]
                alpha = alpha_ref[p, :, start : start + BLOCK]
                scores = jnp.dot(
                    rounded, turned_ref[p, :, start : start + BLOCK], preferred_element_type=F32
                )
                weights = (alpha * scores).astype(BF16)
                if last:
                    squares = squares + weights.astype(F32) * scores
                else:
                    image = image + jnp.dot(weights, items, preferred_element_type=F32)
    if last:
        total = total + jnp.sum(squares, axis=1, keepdims=True)
        msg_ref[...] = row_of(total, msg_ref.shape[0])
    else:
        pack(image, msg_ref)


def final_kernel(n_msgs, *refs):
    msgs = refs[:n_msgs]
    n_ref, d_ref, x_ref, out_ref = refs[n_msgs:]
    direction = d_ref[...]
    total = column_of(tree_sum([m[...] for m in msgs])[:1], 128)
    squares = jnp.sum(direction * direction, axis=1, keepdims=True)
    step_size = n_ref[...] / (total + ridge_weight * squares)
    for at in range(0, direction.shape[1], 128):
        out_ref[:, at : at + 128] = x_ref[:, at : at + 128] + step_size * direction[:, at : at + 128]


def permuted(array, axis, size, target):
    return lax.ppermute(array, axis, [(i, target(i)) for i in range(size)])


def tied(array, token):
    return lax.optimization_barrier((array, token))[0]


def gather_stages(own, size, plan, work):
    send = functools.partial(permuted, axis="row", size=size)
    held = {0: own}
    bit = 8 if size >= 8 else 1
    while bit < size:
        held.update({s ^ bit: send(a, target=lambda i: i ^ bit) for s, a in held.items()})
        bit *= 2
    rows = own.shape[1]
    if size < 8:
        plan([[((s, s), 0, rows) for s in held]])
        work(list(held.values()))
        return

    def twin(array):
        return send(array, target=lambda i: i ^ 1)

    def first_way(array):
        return send(array, target=lambda i: i ^ (2 + 2 * (i & 1)))

    def second_way(array):
        return send(array, target=lambda i: i ^ (4 - 2 * (i & 1)))

    half = rows // 2
    whole, upper, lower = (0, rows), (0, half), (half, half)
    kinds = [
        [((0, 0), *whole), ((1, 1), *whole)],
        [((2, 4), *whole), ((5, 3), *whole), ((4, 2), *whole), ((3, 5), *upper), ((3, 5), *lower)],
        [((6, 6), *whole), ((7, 7), *whole)],
    ]
    early = plan([[((s ^ e, s ^ o), at, n) for s in held for (e, o), at, n in kind] for kind in kinds])

    one = [first_way(a) for a in held.values()]
    two = [second_way(tied(a, early)) for a in held.values()]
    token = work([x for a in held.values() for x in (a, twin(a))])
    one = [tied(a, token) for a in one]
    two = [tied(a, token) for a in two]
    far = [second_way(a) for a in one]
    token = work([x for a, b in zip(one, two) for x in (a, twin(a), b, twin(b[:, :half]), twin(b[:, half:]))])
    far = [tied(a, token) for a in far]
    work([x for a in far for x in (a, twin(a))])


def local(mesh, item_factors, tile_counts, observed_tiles, mask_words, confidence, previous):
    n_row, n_col = mesh.shape["row"], mesh.shape["col"]
    tiles, rows, rank = item_factors.shape
    users, obs, width = mask_words.shape
    slots = rows * n_row
    me = lax.axis_index("row").astype(jnp.int32).reshape(1)
    picks = observed_tiles[0]
    conf = confidence[:, None]
    words = jnp.transpose(mask_words, (1, 0, 2)).astype(BF16)
    shape = jax.ShapeDtypeStruct

    message = shape((users, rank), jnp.int16)
    sums = shape((2, users, rank), F32)
    gram_shape = shape((rank, rank), F32)
    stages, picked, turned, alphas, carry = [], [], [], [], []

    def masks_of(plan):
        for stage in plan:
            spot, pieces = 0, []
            for pair, offset, length in stage:
                pieces.append((spot, pair, offset, length))
                spot += length
            stages.append(pieces)
        sizes = [sum(length for _, _, _, length in pieces) for pieces in stages]
        alphas.extend(
            call(
                functools.partial(masks_kernel, stages, rows),
                [shape((obs, users, size), F32) for size in sizes],
                (me, picks, tile_counts, words, conf),
                3,
                2 * obs * users * sum(sizes) * width,
                "masks",
            )
        )
        return alphas

    def work(arrays):
        index = len(picked)
        first, last = index == 0, index == len(stages) - 1
        pieces, alpha = stages[index], alphas[index]
        size = alpha.shape[2]
        split = shape((rank, rank), BF16)
        kept, kept_turned, *carried = call(
            functools.partial(gather_kernel, pieces, rows, first, last),
            [shape((obs, size, rank), BF16), shape((obs, rank, size), BF16)]
            + ([split, split, message] if last else [gram_shape, sums]),
            (me, picks, tile_counts, alpha, conf, previous, *arrays, *carry),
            3,
            2 * size * rank * (tiles * rank + 3 * obs * users),
            "stage",
        )
        carry[:] = carried
        picked.append(kept)
        turned.append(kept_turned)
        return carried, alphas

    gather_stages(item_factors, n_row, masks_of, work)
    high, low, msg = carry

    def to_all(own):
        return [own] + [permuted(own, "col", n_col, lambda i: i ^ bits) for bits in range(1, n_col)]

    vec = shape((users, rank), F32)
    state = []
    for index in range(ITERS):
        last = index == ITERS - 1
        msgs = to_all(msg)
        outs = [vec] if index == 0 else [vec, vec, vec]
        if last:
            outs = [shape((users, 128), F32), vec, vec]
        outs.append(shape((8, users), F32) if last else message)
        *state, msg = call(
            functools.partial(round_kernel, index, n_col, len(picked)),
            outs,
            (*msgs, previous, high, low, *alphas, *picked, *turned, *state),
            0,
            4 * obs * users * slots * rank,
            f"round{index}",
        )
    msgs = to_all(msg)
    (out,) = pl.pallas_call(
        functools.partial(final_kernel, n_col),
        out_shape=[vec],
        in_specs=[VMEM] * (n_col + 3),
        out_specs=[VMEM],
        compiler_params=pltpu.CompilerParams(vmem_limit_bytes=4 * 1024 * 1024),
        name="final",
    )(*msgs, *state)
    return out


def solution(mesh):
    return jax.shard_map(
        functools.partial(local, mesh),
        mesh=mesh,
        in_specs=(
            P("col", "row", None),
            P("col"),
            P("row", "col"),
            P("row", "col", None),
            P("row"),
            P("row", None),
        ),
        out_specs=P("row", None),
        check_vma=False,
    )
```

```python
import functools

import jax
import jax.numpy as jnp
from jax import lax
from jax.experimental import pallas as pl
from jax.experimental.pallas import tpu as pltpu
from jax.sharding import PartitionSpec as P

ITERS = 3
BLOCK = 256
ridge_weight = 0.1

SMEM = pl.BlockSpec(memory_space=pltpu.SMEM)
VMEM = pl.BlockSpec(memory_space=pltpu.VMEM)
F32 = jnp.float32
BF16 = jnp.bfloat16


def call(body, outs, args, n_smem, flops, name, scalars=()):
    kept = [pltpu.with_memory_space_constraint(a, pltpu.SMEM) for a in args[:n_smem]]
    return pl.pallas_call(
        body,
        out_shape=[pltpu.VMEM(o.shape, o.dtype) for o in outs] + [pltpu.SMEM(o.shape, o.dtype) for o in scalars],
        in_specs=[SMEM] * n_smem + [VMEM] * (len(args) - n_smem),
        out_specs=[VMEM] * len(outs) + [SMEM] * len(scalars),
        compiler_params=pltpu.CompilerParams(vmem_limit_bytes=24 * 1024 * 1024),
        cost_estimate=pl.CostEstimate(flops=flops, bytes_accessed=1 << 20, transcendentals=0),
        name=name,
    )(*kept, *args[n_smem:])


def column_of(row_values, lanes):
    return jnp.broadcast_to(row_values, (lanes, row_values.shape[1])).T


def row_of(column, rows):
    return jnp.broadcast_to(column, (column.shape[0], 128)).T[:rows]


def low_lanes(users):
    lane = lax.broadcasted_iota(jnp.int32, (users, 128), 1)
    return lane, lane < 8


def pack(values, out_ref):
    users, rank = values.shape
    top = jnp.max(jnp.abs(values), axis=1, keepdims=True)
    power = jnp.clip(jnp.ceil(jnp.log2(jnp.maximum(top, 1e-30))), -100.0, 127.0)
    scaled = jnp.round(values * jnp.exp2(15.0 - power))
    scaled = jnp.clip(scaled, -32767.0, 32767.0).astype(jnp.int32)
    lane, low = low_lanes(users)
    bit = jnp.right_shift(jnp.broadcast_to((power + 128.0).astype(jnp.int32), lane.shape), lane & 7) & 1
    head = scaled[:, :128]
    out_ref[:, :128] = jnp.where(low, (head & -2) | bit, head).astype(jnp.int16)
    out_ref[:, 128:] = scaled[:, 128:].astype(jnp.int16)


def unpack(ref):
    users = ref.shape[0]
    whole = ref[...].astype(jnp.int32)
    head = whole[:, :128]
    lane, low = low_lanes(users)
    bit = jnp.where(low, head & 1, 0)
    power = jnp.sum(jnp.left_shift(bit, lane & 7).astype(F32), axis=1, keepdims=True) - 128.0
    whole = jnp.concatenate([head - bit, whole[:, 128:]], axis=1)
    return whole.astype(F32) * jnp.exp2(power - 15.0)


def tree_sum(parts):
    while len(parts) > 1:
        parts = [parts[i] + parts[i + 1] for i in range(0, len(parts), 2)]
    return parts[0]


def shard_index(me, shards):
    even, odd = shards
    return me ^ (even + (me & 1) * (odd - even))


def masks_kernel(stages, rows, info_ref, words_ref, conf_ref, *out_refs):
    *out_refs, kept_ref = out_refs
    for index in range(info_ref.shape[0]):
        kept_ref[index] = info_ref[index]
    me = info_ref[0]
    obs, _, width = words_ref.shape
    lane = lax.broadcasted_iota(jnp.int32, (1, BLOCK), 1)
    word_index = lax.broadcasted_iota(jnp.int32, (width, BLOCK), 0)
    for pieces, out_ref in zip(stages, out_refs):
        for at in range(0, out_ref.shape[2], BLOCK):
            slot = jnp.zeros((1, BLOCK), jnp.int32)
            for spot, pair, offset, _ in pieces:
                if at <= spot < at + BLOCK:
                    start = shard_index(me, pair) * rows + offset - (spot - at)
                    slot = jnp.where(lane >= spot - at, lane + start, slot)
            spread = (word_index == jnp.right_shift(slot, 3)).astype(BF16)
            for p in range(obs):
                count = info_ref[1 + obs + info_ref[1 + p]]
                word = jnp.dot(words_ref[p], spread, preferred_element_type=F32).astype(jnp.int32)
                bits = jnp.right_shift(word, slot & 7) & 1
                bits = jnp.where(slot < count, bits, 0).astype(F32)
                out_ref[p, :, at : at + BLOCK] = bits * conf_ref[...]


def gather_kernel(pieces, rows, first, last, *refs):
    info_ref, alpha_ref, conf_ref, prev_ref = refs[:4]
    at = 4
    arrays = refs[at : at + len(pieces)]
    at += len(pieces)
    if not first:
        gram_in, sums_in = refs[at : at + 2]
        at += 2
    picked_ref, turned_ref = refs[at : at + 2]
    at += 2
    if last:
        high_ref, low_ref, msg_ref = refs[at:]
    else:
        gram_ref, sums_ref = refs[at:]
    me = info_ref[0]
    users, rank = prev_ref.shape
    obs = alpha_ref.shape[0]
    tiles = arrays[0].shape[0]
    for p in range(obs):
        tile = info_ref[1 + p]
        for (spot, _, _, length), ref in zip(pieces, arrays):
            picked_ref[p, spot : spot + length, :] = ref[tile]
    gram = jnp.zeros((rank, rank), F32) if first else gram_in[...]
    for (_, pair, offset, length), ref in zip(pieces, arrays):
        slot = lax.broadcasted_iota(jnp.int32, (length, rank), 0)
        slot = slot + (shard_index(me, pair) * rows + offset)
        for t in range(tiles):
            tile_rows = ref[t]
            masked = jnp.where(slot < info_ref[1 + obs + t], tile_rows, jnp.zeros_like(tile_rows))
            gram = gram + lax.dot_general(
                masked, tile_rows, (((0,), (0,)), ((), ())), preferred_element_type=F32
            )
    if last:
        high = gram.astype(BF16)
        low = (gram - high.astype(F32)).astype(BF16)
        high_ref[...] = high
        low_ref[...] = low
    else:
        gram_ref[...] = gram
    prev = prev_ref[...]
    rhs = jnp.zeros((users, rank), F32) if first else sums_in[0]
    image = jnp.zeros((users, rank), F32) if first else sums_in[1]
    for p in range(obs):
        for start in range(0, picked_ref.shape[1], BLOCK):
            items = picked_ref[p, start : start + BLOCK, :]
            turned = items.T
            turned_ref[p, :, start : start + BLOCK] = turned
            alpha = alpha_ref[p, :, start : start + BLOCK]
            scores = jnp.dot(prev, turned, preferred_element_type=F32)
            weights = (alpha * scores).astype(BF16)
            seen = jnp.where(alpha > 0.0, 1.0, 0.0).astype(BF16)
            rhs = rhs + jnp.dot(seen, items, preferred_element_type=F32)
            image = image + jnp.dot(weights, items, preferred_element_type=F32)
    if last:
        image = image + jnp.dot(prev, high, preferred_element_type=F32)
        image = image + jnp.dot(prev, low, preferred_element_type=F32)
        pack((1.0 + conf_ref[...]) * rhs - image, msg_ref)
    else:
        sums_ref[0] = rhs
        sums_ref[1] = image


def in_order(refs, order):
    return [refs[order.index(bits)] for bits in range(len(order))]


def round_kernel(step_index, order, n_stages, *refs):
    msgs = in_order(refs, order)
    refs = refs[len(order) :]
    prev_ref, high_ref, low_ref = refs[:3]
    alphas, picked, turned = (refs[3 + n * n_stages : 3 + (n + 1) * n_stages] for n in range(3))
    refs = refs[3 + 3 * n_stages :]
    summed = tree_sum([unpack(m) for m in msgs])
    if step_index == 0:
        (r_ref, msg_ref) = refs
        residual = summed - ridge_weight * prev_ref[...].astype(F32)
        direction = residual
        r_ref[...] = residual
    else:
        n_state = 1 if step_index == 1 else 3
        state = refs[:n_state]
        refs = refs[n_state:]
        if step_index == 1:
            residual = direction = state[0][...]
            solution = prev_ref[...].astype(F32)
        else:
            residual, direction, solution = (s[...] for s in state)
        image = summed + ridge_weight * direction
        norm_now = jnp.sum(residual * residual, axis=1, keepdims=True)
        step_size = norm_now / jnp.sum(direction * image, axis=1, keepdims=True)
        solution = solution + step_size * direction
        residual = residual - step_size * image
        norm_next = jnp.sum(residual * residual, axis=1, keepdims=True)
        direction = residual + (norm_next / norm_now) * direction
        if step_index < ITERS - 1:
            r_ref, d_ref, x_ref, msg_ref = refs
            r_ref[...] = residual
        else:
            n_ref, d_ref, x_ref, msg_ref = refs
            n_ref[...] = jnp.broadcast_to(norm_next, n_ref.shape)
        d_ref[...] = direction
        x_ref[...] = solution
    last = step_index == ITERS - 1
    rounded = direction.astype(BF16)
    users = direction.shape[0]
    both = jnp.concatenate([rounded, (direction - rounded.astype(F32)).astype(BF16)], axis=0)
    both = jnp.dot(both, high_ref[...], preferred_element_type=F32)
    image = both[:users] + both[users:] + jnp.dot(rounded, low_ref[...], preferred_element_type=F32)
    if last:
        total = jnp.sum(image * direction, axis=1, keepdims=True)
        squares = jnp.zeros((direction.shape[0], BLOCK), F32)
    for alpha_ref, ref, turned_ref in zip(alphas, picked, turned):
        for p in range(ref.shape[0]):
            for start in range(0, ref.shape[1], BLOCK):
                items = ref[p, start : start + BLOCK, :]
                alpha = alpha_ref[p, :, start : start + BLOCK]
                scores = jnp.dot(
                    rounded, turned_ref[p, :, start : start + BLOCK], preferred_element_type=F32
                )
                weights = (alpha * scores).astype(BF16)
                if last:
                    squares = squares + weights.astype(F32) * scores
                else:
                    image = image + jnp.dot(weights, items, preferred_element_type=F32)
    if last:
        total = total + jnp.sum(squares, axis=1, keepdims=True)
        msg_ref[...] = row_of(total, msg_ref.shape[0])
    else:
        pack(image, msg_ref)


def final_kernel(order, *refs):
    msgs = in_order(refs, order)
    n_ref, d_ref, x_ref, out_ref = refs[len(order) :]
    direction = d_ref[...]
    total = column_of(tree_sum([m[...] for m in msgs])[:1], 128)
    squares = jnp.sum(direction * direction, axis=1, keepdims=True)
    step_size = n_ref[...] / (total + ridge_weight * squares)
    for at in range(0, direction.shape[1], 128):
        out_ref[:, at : at + 128] = x_ref[:, at : at + 128] + step_size * direction[:, at : at + 128]


def permuted(array, axis, size, target):
    return lax.ppermute(array, axis, [(i, target(i)) for i in range(size)])


def tied(array, token):
    return lax.optimization_barrier((array, token))[0]


def gather_stages(own, size, plan, work):
    send = functools.partial(permuted, axis="row", size=size)
    held = {0: own}
    bit = 8 if size >= 8 else 1
    while bit < size:
        held.update({s ^ bit: send(a, target=lambda i: i ^ bit) for s, a in held.items()})
        bit *= 2
    rows = own.shape[1]
    if size < 8:
        plan([[((s, s), 0, rows) for s in held]])
        work(list(held.values()))
        return

    def twin(array):
        return send(array, target=lambda i: i ^ 1)

    def first_way(array):
        return send(array, target=lambda i: i ^ (2 + 2 * (i & 1)))

    def second_way(array):
        return send(array, target=lambda i: i ^ (4 - 2 * (i & 1)))

    half = rows // 2
    whole, upper, lower = (0, rows), (0, half), (half, half)
    kinds = [
        [((0, 0), *whole), ((1, 1), *whole)],
        [((2, 4), *whole), ((5, 3), *upper), ((5, 3), *lower), ((4, 2), *whole), ((3, 5), *upper), ((3, 5), *lower)],
        [((6, 6), *whole)],
        [((7, 7), *whole)],
    ]
    early = plan([[((s ^ e, s ^ o), at, n) for s in held for (e, o), at, n in kind] for kind in kinds])

    one = [first_way(a) for a in held.values()]
    two = [second_way(tied(a, early)) for a in held.values()]
    token = work([x for a in held.values() for x in (a, twin(a))])
    one = [tied(a, token) for a in one]
    two = [tied(a, token) for a in two]
    far = [second_way(a) for a in one]
    token = work([x for a, b in zip(one, two) for x in (a, twin(a[:, :half]), twin(a[:, half:]), b, twin(b[:, :half]), twin(b[:, half:]))])
    far = [tied(a, token) for a in far]
    work(far)
    work([twin(a) for a in far])


def local(mesh, item_factors, tile_counts, observed_tiles, mask_words, confidence, previous):
    n_row, n_col = mesh.shape["row"], mesh.shape["col"]
    tiles, rows, rank = item_factors.shape
    users, obs, width = mask_words.shape
    slots = rows * n_row
    me = lax.axis_index("row").astype(jnp.int32).reshape(1)
    info = jnp.concatenate([me, observed_tiles[0], tile_counts])
    conf = confidence[:, None]
    words = jnp.transpose(mask_words, (1, 0, 2)).astype(BF16)
    shape = jax.ShapeDtypeStruct

    message = shape((users, rank), jnp.int16)
    sums = shape((2, users, rank), F32)
    gram_shape = shape((rank, rank), F32)
    stages, picked, turned, alphas, carry, scalars = [], [], [], [], [], []

    def masks_of(plan):
        for stage in plan:
            spot, pieces = 0, []
            for pair, offset, length in stage:
                pieces.append((spot, pair, offset, length))
                spot += length
            stages.append(pieces)
        sizes = [sum(length for _, _, _, length in pieces) for pieces in stages]
        *masks, kept_info = (
            call(
                functools.partial(masks_kernel, stages, rows),
                [shape((obs, users, size), F32) for size in sizes],
                (info, words, conf),
                1,
                2 * obs * users * sum(sizes) * width,
                "masks",
                [shape(info.shape, info.dtype)],
            )
        )
        alphas.extend(masks)
        scalars.append(kept_info)
        return alphas

    def work(arrays):
        index = len(picked)
        first, last = index == 0, index == len(stages) - 1
        pieces, alpha = stages[index], alphas[index]
        size = alpha.shape[2]
        split = shape((rank, rank), BF16)
        kept, kept_turned, *carried = call(
            functools.partial(gather_kernel, pieces, rows, first, last),
            [shape((obs, size, rank), BF16), shape((obs, rank, size), BF16)]
            + ([split, split, message] if last else [gram_shape, sums]),
            (*scalars, alpha, conf, previous, *arrays, *carry),
            1,
            2 * size * rank * (tiles * rank + 3 * obs * users),
            "stage",
        )
        carry[:] = carried
        picked.append(kept)
        turned.append(kept_turned)
        return carried, alphas

    gather_stages(item_factors, n_row, masks_of, work)
    high, low, msg = carry

    order = [0, *range(2, n_col, 2), *range(1, n_col, 2)]

    def to_all(own):
        return [own] + [permuted(own, "col", n_col, lambda i: i ^ bits) for bits in order[1:]]

    vec = shape((users, rank), F32)
    state = []
    for index in range(ITERS):
        last = index == ITERS - 1
        msgs = to_all(msg)
        outs = [vec] if index == 0 else [vec, vec, vec]
        if last:
            outs = [shape((users, 128), F32), vec, vec]
        outs.append(shape((8, users), F32) if last else message)
        *state, msg = call(
            functools.partial(round_kernel, index, order, len(picked)),
            outs,
            (*msgs, previous, high, low, *alphas, *picked, *turned, *state),
            0,
            4 * obs * users * slots * rank,
            f"round{index}",
        )
    msgs = to_all(msg)
    (out,) = pl.pallas_call(
        functools.partial(final_kernel, order),
        out_shape=[vec],
        in_specs=[VMEM] * (n_col + 3),
        out_specs=[VMEM],
        compiler_params=pltpu.CompilerParams(vmem_limit_bytes=4 * 1024 * 1024),
        name="final",
    )(*msgs, *state)
    return out


def solution(mesh):
    return jax.shard_map(
        functools.partial(local, mesh),
        mesh=mesh,
        in_specs=(
            P("col", "row", None),
            P("col"),
            P("row", "col"),
            P("row", "col", None),
            P("row"),
            P("row", None),
        ),
        out_specs=P("row", None),
        check_vma=False,
    )
```

```python
import functools

import jax
import jax.numpy as jnp
from jax import lax
from jax.experimental import pallas as pl
from jax.experimental.pallas import tpu as pltpu
from jax.sharding import PartitionSpec as P

ITERS = 3
BLOCK = 256
ridge_weight = 0.1

SMEM = pl.BlockSpec(memory_space=pltpu.SMEM)
VMEM = pl.BlockSpec(memory_space=pltpu.VMEM)
F32 = jnp.float32
BF16 = jnp.bfloat16


def call(body, outs, args, n_smem, flops, name, scalars=()):
    kept = [pltpu.with_memory_space_constraint(a, pltpu.SMEM) for a in args[:n_smem]]
    return pl.pallas_call(
        body,
        out_shape=[pltpu.VMEM(o.shape, o.dtype) for o in outs] + [pltpu.SMEM(o.shape, o.dtype) for o in scalars],
        in_specs=[SMEM] * n_smem + [VMEM] * (len(args) - n_smem),
        out_specs=[VMEM] * len(outs) + [SMEM] * len(scalars),
        compiler_params=pltpu.CompilerParams(vmem_limit_bytes=24 * 1024 * 1024),
        cost_estimate=pl.CostEstimate(flops=flops, bytes_accessed=1 << 20, transcendentals=0),
        name=name,
    )(*kept, *args[n_smem:])


def column_of(row_values, lanes):
    return jnp.broadcast_to(row_values, (lanes, row_values.shape[1])).T


def row_of(column, rows):
    return jnp.broadcast_to(column, (column.shape[0], 128)).T[:rows]


def low_lanes(users):
    lane = lax.broadcasted_iota(jnp.int32, (users, 128), 1)
    return lane, lane < 8


def pack(values, out_ref):
    users, rank = values.shape
    top = jnp.max(jnp.abs(values), axis=1, keepdims=True)
    power = jnp.clip(jnp.ceil(jnp.log2(jnp.maximum(top, 1e-30))), -100.0, 127.0)
    scaled = jnp.round(values * jnp.exp2(15.0 - power))
    scaled = jnp.clip(scaled, -32767.0, 32767.0).astype(jnp.int32)
    lane, low = low_lanes(users)
    bit = jnp.right_shift(jnp.broadcast_to((power + 128.0).astype(jnp.int32), lane.shape), lane & 7) & 1
    head = scaled[:, :128]
    out_ref[:, :128] = jnp.where(low, (head & -2) | bit, head).astype(jnp.int16)
    out_ref[:, 128:] = scaled[:, 128:].astype(jnp.int16)


def unpack(ref):
    users = ref.shape[0]
    whole = ref[...].astype(jnp.int32)
    head = whole[:, :128]
    lane, low = low_lanes(users)
    bit = jnp.where(low, head & 1, 0)
    power = jnp.sum(jnp.left_shift(bit, lane & 7).astype(F32), axis=1, keepdims=True) - 128.0
    whole = jnp.concatenate([head - bit, whole[:, 128:]], axis=1)
    return whole.astype(F32) * jnp.exp2(power - 15.0)


def blocks(size):
    return [slice(at, min(at + BLOCK, size)) for at in range(0, size, BLOCK)]


def tree_sum(parts):
    while len(parts) > 1:
        parts = [parts[i] + parts[i + 1] for i in range(0, len(parts), 2)]
    return parts[0]


def shard_index(me, shards):
    even, odd = shards
    return me ^ (even + (me & 1) * (odd - even))


def masks_kernel(stages, rows, info_ref, words_ref, conf_ref, *out_refs):
    *out_refs, kept_ref = out_refs
    for index in range(info_ref.shape[0]):
        kept_ref[index] = info_ref[index]
    me = info_ref[0]
    obs, _, width = words_ref.shape
    for pieces, out_ref in zip(stages, out_refs):
        for block in blocks(out_ref.shape[2]):
            size = block.stop - block.start
            lane = lax.broadcasted_iota(jnp.int32, (1, size), 1)
            slot = jnp.zeros((1, size), jnp.int32)
            for spot, pair, offset, _ in pieces:
                place = spot - block.start
                if 0 <= place < size:
                    start = shard_index(me, pair) * rows + offset - place
                    slot = jnp.where(lane >= place, lane + start, slot)
            word_index = lax.broadcasted_iota(jnp.int32, (width, size), 0)
            spread = (word_index == jnp.right_shift(slot, 3)).astype(BF16)
            for p in range(obs):
                count = info_ref[1 + obs + info_ref[1 + p]]
                word = jnp.dot(words_ref[p], spread, preferred_element_type=F32).astype(jnp.int32)
                bits = jnp.right_shift(word, slot & 7) & 1
                bits = jnp.where(slot < count, bits, 0).astype(F32)
                out_ref[p, :, block] = bits * conf_ref[...]


def gather_kernel(pieces, rows, first, last, *refs):
    info_ref, alpha_ref, conf_ref, prev_ref = refs[:4]
    at = 4
    arrays = refs[at : at + len(pieces)]
    at += len(pieces)
    if not first:
        gram_in, sums_in = refs[at : at + 2]
        at += 2
    picked_ref, turned_ref = refs[at : at + 2]
    at += 2
    if last:
        high_ref, low_ref, msg_ref = refs[at:]
    else:
        gram_ref, sums_ref = refs[at:]
    me = info_ref[0]
    users, rank = prev_ref.shape
    obs = alpha_ref.shape[0]
    tiles = arrays[0].shape[0]
    for p in range(obs):
        tile = info_ref[1 + p]
        for (spot, _, _, length), ref in zip(pieces, arrays):
            picked_ref[p, spot : spot + length, :] = ref[tile]
    gram = jnp.zeros((rank, rank), F32) if first else gram_in[...]
    for (_, pair, offset, length), ref in zip(pieces, arrays):
        slot = lax.broadcasted_iota(jnp.int32, (length, rank), 0)
        slot = slot + (shard_index(me, pair) * rows + offset)
        for t in range(tiles):
            tile_rows = ref[t]
            masked = jnp.where(slot < info_ref[1 + obs + t], tile_rows, jnp.zeros_like(tile_rows))
            gram = gram + lax.dot_general(
                masked, tile_rows, (((0,), (0,)), ((), ())), preferred_element_type=F32
            )
    if last:
        high = gram.astype(BF16)
        low = (gram - high.astype(F32)).astype(BF16)
        high_ref[...] = high
        low_ref[...] = low
    else:
        gram_ref[...] = gram
    prev = prev_ref[...]
    rhs = jnp.zeros((users, rank), F32) if first else sums_in[0]
    image = jnp.zeros((users, rank), F32) if first else sums_in[1]
    for p in range(obs):
        for block in blocks(picked_ref.shape[1]):
            items = picked_ref[p, block, :]
            turned = items.T
            turned_ref[p, :, block] = turned
            alpha = alpha_ref[p, :, block]
            scores = jnp.dot(prev, turned, preferred_element_type=F32)
            weights = (alpha * scores).astype(BF16)
            seen = jnp.where(alpha > 0.0, 1.0, 0.0).astype(BF16)
            rhs = rhs + jnp.dot(seen, items, preferred_element_type=F32)
            image = image + jnp.dot(weights, items, preferred_element_type=F32)
    if last:
        image = image + jnp.dot(prev, high, preferred_element_type=F32)
        image = image + jnp.dot(prev, low, preferred_element_type=F32)
        pack((1.0 + conf_ref[...]) * rhs - image, msg_ref)
    else:
        sums_ref[0] = rhs
        sums_ref[1] = image


def in_order(refs, order):
    return [refs[order.index(bits)] for bits in range(len(order))]


def round_kernel(step_index, order, n_stages, *refs):
    msgs = in_order(refs, order)
    refs = refs[len(order) :]
    prev_ref, high_ref, low_ref = refs[:3]
    alphas, picked, turned = (refs[3 + n * n_stages : 3 + (n + 1) * n_stages] for n in range(3))
    refs = refs[3 + 3 * n_stages :]
    summed = tree_sum([unpack(m) for m in msgs])
    if step_index == 0:
        (r_ref, msg_ref) = refs
        residual = summed - ridge_weight * prev_ref[...].astype(F32)
        direction = residual
        r_ref[...] = residual
    else:
        n_state = 1 if step_index == 1 else 3
        state = refs[:n_state]
        refs = refs[n_state:]
        if step_index == 1:
            residual = direction = state[0][...]
            solution = prev_ref[...].astype(F32)
        else:
            residual, direction, solution = (s[...] for s in state)
        image = summed + ridge_weight * direction
        norm_now = jnp.sum(residual * residual, axis=1, keepdims=True)
        step_size = norm_now / jnp.sum(direction * image, axis=1, keepdims=True)
        solution = solution + step_size * direction
        residual = residual - step_size * image
        norm_next = jnp.sum(residual * residual, axis=1, keepdims=True)
        direction = residual + (norm_next / norm_now) * direction
        if step_index < ITERS - 1:
            r_ref, d_ref, x_ref, msg_ref = refs
            r_ref[...] = residual
        else:
            n_ref, d_ref, x_ref, msg_ref = refs
            n_ref[...] = jnp.broadcast_to(norm_next, n_ref.shape)
        d_ref[...] = direction
        x_ref[...] = solution
    last = step_index == ITERS - 1
    rounded = direction.astype(BF16)
    users = direction.shape[0]
    both = jnp.concatenate([rounded, (direction - rounded.astype(F32)).astype(BF16)], axis=0)
    both = jnp.dot(both, high_ref[...], preferred_element_type=F32)
    image = both[:users] + both[users:] + jnp.dot(rounded, low_ref[...], preferred_element_type=F32)
    if last:
        total = jnp.sum(image * direction, axis=1, keepdims=True)
    for alpha_ref, ref, turned_ref in zip(alphas, picked, turned):
        for p in range(ref.shape[0]):
            for block in blocks(ref.shape[1]):
                items = ref[p, block, :]
                alpha = alpha_ref[p, :, block]
                scores = jnp.dot(rounded, turned_ref[p, :, block], preferred_element_type=F32)
                weights = (alpha * scores).astype(BF16)
                if last:
                    total = total + jnp.sum(weights.astype(F32) * scores, axis=1, keepdims=True)
                else:
                    image = image + jnp.dot(weights, items, preferred_element_type=F32)
    if last:
        msg_ref[...] = row_of(total, msg_ref.shape[0])
    else:
        pack(image, msg_ref)


def final_kernel(order, *refs):
    msgs = in_order(refs, order)
    n_ref, d_ref, x_ref, out_ref = refs[len(order) :]
    direction = d_ref[...]
    total = column_of(tree_sum([m[...] for m in msgs])[:1], 128)
    squares = jnp.sum(direction * direction, axis=1, keepdims=True)
    step_size = n_ref[...] / (total + ridge_weight * squares)
    for at in range(0, direction.shape[1], 128):
        out_ref[:, at : at + 128] = x_ref[:, at : at + 128] + step_size * direction[:, at : at + 128]


def permuted(array, axis, size, target):
    return lax.ppermute(array, axis, [(i, target(i)) for i in range(size)])


def tied(array, token):
    return lax.optimization_barrier((array, token))[0]


def gather_stages(own, size, plan, work):
    send = functools.partial(permuted, axis="row", size=size)
    held = {0: own}
    bit = 8 if size >= 8 else 1
    while bit < size:
        held.update({s ^ bit: send(a, target=lambda i: i ^ bit) for s, a in held.items()})
        bit *= 2
    rows = own.shape[1]
    if size < 8:
        plan([[((s, s), 0, rows) for s in held]])
        work(list(held.values()))
        return

    def twin(array):
        return send(array, target=lambda i: i ^ 1)

    def first_way(array):
        return send(array, target=lambda i: i ^ (2 + 2 * (i & 1)))

    def second_way(array):
        return send(array, target=lambda i: i ^ (4 - 2 * (i & 1)))

    half = rows // 2
    whole, upper, lower = (0, rows), (0, half), (half, half)
    kinds = [
        [((0, 0), *whole), ((1, 1), *whole)],
        [((2, 4), *whole), ((5, 3), *upper), ((5, 3), *lower), ((4, 2), *whole), ((3, 5), *upper), ((3, 5), *lower)],
        [((6, 6), *whole)],
        [((7, 7), *whole)],
    ]
    early = plan([[((s ^ e, s ^ o), at, n) for s in held for (e, o), at, n in kind] for kind in kinds])

    one = [first_way(a) for a in held.values()]
    two = [second_way(tied(a, early)) for a in held.values()]
    token = work([x for a in held.values() for x in (a, twin(a))])
    one = [tied(a, token) for a in one]
    two = [tied(a, token) for a in two]
    far = [second_way(a) for a in one]
    token = work([x for a, b in zip(one, two) for x in (a, twin(a[:, :half]), twin(a[:, half:]), b, twin(b[:, :half]), twin(b[:, half:]))])
    far = [tied(a, token) for a in far]
    work(far)
    work([twin(a) for a in far])


def local(mesh, item_factors, tile_counts, observed_tiles, mask_words, confidence, previous):
    n_row, n_col = mesh.shape["row"], mesh.shape["col"]
    tiles, rows, rank = item_factors.shape
    users, obs, width = mask_words.shape
    slots = rows * n_row
    me = lax.axis_index("row").astype(jnp.int32).reshape(1)
    info = jnp.concatenate([me, observed_tiles[0], tile_counts])
    conf = confidence[:, None]
    words = jnp.transpose(mask_words, (1, 0, 2)).astype(BF16)
    shape = jax.ShapeDtypeStruct

    message = shape((users, rank), jnp.int16)
    sums = shape((2, users, rank), F32)
    gram_shape = shape((rank, rank), F32)
    stages, picked, turned, alphas, carry, scalars = [], [], [], [], [], []

    def masks_of(plan):
        for stage in plan:
            spot, pieces = 0, []
            for pair, offset, length in stage:
                pieces.append((spot, pair, offset, length))
                spot += length
            stages.append(pieces)
        sizes = [sum(length for _, _, _, length in pieces) for pieces in stages]
        *masks, kept_info = (
            call(
                functools.partial(masks_kernel, stages, rows),
                [shape((obs, users, size), F32) for size in sizes],
                (info, words, conf),
                1,
                2 * obs * users * sum(sizes) * width,
                "masks",
                [shape(info.shape, info.dtype)],
            )
        )
        alphas.extend(masks)
        scalars.append(kept_info)
        return alphas

    def work(arrays):
        index = len(picked)
        first, last = index == 0, index == len(stages) - 1
        pieces, alpha = stages[index], alphas[index]
        size = alpha.shape[2]
        split = shape((rank, rank), BF16)
        kept, kept_turned, *carried = call(
            functools.partial(gather_kernel, pieces, rows, first, last),
            [shape((obs, size, rank), BF16), shape((obs, rank, size), BF16)]
            + ([split, split, message] if last else [gram_shape, sums]),
            (*scalars, alpha, conf, previous, *arrays, *carry),
            1,
            2 * size * rank * (tiles * rank + 3 * obs * users),
            "stage",
        )
        carry[:] = carried
        picked.append(kept)
        turned.append(kept_turned)
        return carried, alphas

    gather_stages(item_factors, n_row, masks_of, work)
    high, low, msg = carry

    order = [0, *range(2, n_col, 2), *range(1, n_col, 2)]

    def to_all(own):
        return [own] + [permuted(own, "col", n_col, lambda i: i ^ bits) for bits in order[1:]]

    vec = shape((users, rank), F32)
    state = []
    for index in range(ITERS):
        last = index == ITERS - 1
        msgs = to_all(msg)
        outs = [vec] if index == 0 else [vec, vec, vec]
        if last:
            outs = [shape((users, 128), F32), vec, vec]
        outs.append(shape((8, users), F32) if last else message)
        *state, msg = call(
            functools.partial(round_kernel, index, order, len(picked)),
            outs,
            (*msgs, previous, high, low, *alphas, *picked, *turned, *state),
            0,
            4 * obs * users * slots * rank,
            f"round{index}",
        )
    msgs = to_all(msg)
    (out,) = pl.pallas_call(
        functools.partial(final_kernel, order),
        out_shape=[vec],
        in_specs=[VMEM] * (n_col + 3),
        out_specs=[VMEM],
        compiler_params=pltpu.CompilerParams(vmem_limit_bytes=4 * 1024 * 1024),
        name="final",
    )(*msgs, *state)
    return out


def solution(mesh):
    return jax.shard_map(
        functools.partial(local, mesh),
        mesh=mesh,
        in_specs=(
            P("col", "row", None),
            P("col"),
            P("row", "col"),
            P("row", "col", None),
            P("row"),
            P("row", None),
        ),
        out_specs=P("row", None),
        check_vma=False,
    )
```

```python
import functools

import jax
import jax.numpy as jnp
from jax import lax
from jax.experimental import pallas as pl
from jax.experimental.pallas import tpu as pltpu
from jax.sharding import PartitionSpec as P

ITERS = 3
BLOCK = 256
ridge_weight = 0.1

SMEM = pl.BlockSpec(memory_space=pltpu.SMEM)
VMEM = pl.BlockSpec(memory_space=pltpu.VMEM)
F32 = jnp.float32
BF16 = jnp.bfloat16


def call(body, outs, args, n_smem, flops, name, scalars=()):
    kept = [pltpu.with_memory_space_constraint(a, pltpu.SMEM) for a in args[:n_smem]]
    return pl.pallas_call(
        body,
        out_shape=[pltpu.VMEM(o.shape, o.dtype) for o in outs] + [pltpu.SMEM(o.shape, o.dtype) for o in scalars],
        in_specs=[SMEM] * n_smem + [VMEM] * (len(args) - n_smem),
        out_specs=[VMEM] * len(outs) + [SMEM] * len(scalars),
        compiler_params=pltpu.CompilerParams(vmem_limit_bytes=24 * 1024 * 1024),
        cost_estimate=pl.CostEstimate(flops=flops, bytes_accessed=1 << 20, transcendentals=0),
        name=name,
    )(*kept, *args[n_smem:])


def column_of(row_values, lanes):
    return jnp.broadcast_to(row_values, (lanes, row_values.shape[1])).T


def row_of(column, rows):
    return jnp.broadcast_to(column, (column.shape[0], 128)).T[:rows]


def low_lanes(users):
    lane = lax.broadcasted_iota(jnp.int32, (users, 128), 1)
    return lane, lane < 8


def pack(values, out_ref):
    users, rank = values.shape
    top = jnp.max(jnp.abs(values), axis=1, keepdims=True)
    power = jnp.clip(jnp.ceil(jnp.log2(jnp.maximum(top, 1e-30))), -100.0, 127.0)
    scaled = jnp.round(values * jnp.exp2(15.0 - power))
    scaled = jnp.clip(scaled, -32767.0, 32767.0).astype(jnp.int32)
    lane, low = low_lanes(users)
    bit = jnp.right_shift(jnp.broadcast_to((power + 128.0).astype(jnp.int32), lane.shape), lane & 7) & 1
    head = scaled[:, :128]
    out_ref[:, :128] = jnp.where(low, (head & -2) | bit, head).astype(jnp.int16)
    out_ref[:, 128:] = scaled[:, 128:].astype(jnp.int16)


def unpack(ref):
    users = ref.shape[0]
    whole = ref[...].astype(jnp.int32)
    head = whole[:, :128]
    lane, low = low_lanes(users)
    bit = jnp.where(low, head & 1, 0)
    power = jnp.sum(jnp.left_shift(bit, lane & 7).astype(F32), axis=1, keepdims=True) - 128.0
    whole = jnp.concatenate([head - bit, whole[:, 128:]], axis=1)
    return whole.astype(F32) * jnp.exp2(power - 15.0)


def blocks(size):
    return [slice(at, min(at + BLOCK, size)) for at in range(0, size, BLOCK)]


def tree_sum(parts):
    while len(parts) > 1:
        parts = [parts[i] + parts[i + 1] for i in range(0, len(parts), 2)]
    return parts[0]


def shard_index(me, shards):
    even, odd = shards
    return me ^ (even + (me & 1) * (odd - even))


def masks_kernel(stages, rows, info_ref, words_ref, conf_ref, *out_refs):
    *out_refs, kept_ref = out_refs
    for index in range(info_ref.shape[0]):
        kept_ref[index] = info_ref[index]
    me = info_ref[0]
    obs, _, width = words_ref.shape
    for pieces, out_ref in zip(stages, out_refs):
        for block in blocks(out_ref.shape[2]):
            size = block.stop - block.start
            lane = lax.broadcasted_iota(jnp.int32, (1, size), 1)
            slot = jnp.zeros((1, size), jnp.int32)
            for spot, pair, offset, _ in pieces:
                place = spot - block.start
                if 0 <= place < size:
                    start = shard_index(me, pair) * rows + offset - place
                    slot = jnp.where(lane >= place, lane + start, slot)
            word_index = lax.broadcasted_iota(jnp.int32, (width, size), 0)
            spread = (word_index == jnp.right_shift(slot, 3)).astype(BF16)
            for p in range(obs):
                count = info_ref[1 + obs + info_ref[1 + p]]
                word = jnp.dot(words_ref[p], spread, preferred_element_type=F32).astype(jnp.int32)
                bits = jnp.right_shift(word, slot & 7) & 1
                bits = jnp.where(slot < count, bits, 0).astype(F32)
                out_ref[p, :, block] = bits * conf_ref[...]


def gather_kernel(pieces, rows, first, last, closing, *refs):
    info_ref, alpha_ref, conf_ref, prev_ref = refs[:4]
    at = 4
    arrays = refs[at : at + len(pieces)]
    at += len(pieces)
    if not first:
        gram_in, sums_in = refs[at : at + 2]
        at += 2
    picked_ref, turned_ref = refs[at : at + 2]
    at += 2
    if last:
        high_ref, low_ref, msg_ref = refs[at:]
    else:
        gram_ref, sums_ref = refs[at:]
    me = info_ref[0]
    users, rank = prev_ref.shape
    obs = alpha_ref.shape[0]
    tiles = arrays[0].shape[0]
    for p in range(obs):
        tile = info_ref[1 + p]
        for (spot, _, _, length), ref in zip(pieces, arrays):
            picked_ref[p, spot : spot + length, :] = ref[tile]
    gram = jnp.zeros((rank, rank), F32) if first else gram_in[...]
    for (_, pair, offset, length), ref in zip(pieces, arrays):
        slot = lax.broadcasted_iota(jnp.int32, (length, rank), 0)
        slot = slot + (shard_index(me, pair) * rows + offset)
        for t in range(tiles):
            tile_rows = ref[t]
            masked = jnp.where(slot < info_ref[1 + obs + t], tile_rows, jnp.zeros_like(tile_rows))
            gram = gram + lax.dot_general(
                masked, tile_rows, (((0,), (0,)), ((), ())), preferred_element_type=F32
            )
    if last:
        high = gram.astype(BF16)
        low = (gram - high.astype(F32)).astype(BF16)
        high_ref[...] = high
        low_ref[...] = low
    else:
        gram_ref[...] = gram
    prev = prev_ref[...]
    rhs = jnp.zeros((users, rank), F32) if first else sums_in[0]
    image = jnp.zeros((users, rank), F32) if first else sums_in[1]
    for p in range(obs):
        for block in blocks(picked_ref.shape[1]):
            items = picked_ref[p, block, :]
            turned = items.T
            turned_ref[p, :, block] = turned
            alpha = alpha_ref[p, :, block]
            scores = jnp.dot(prev, turned, preferred_element_type=F32)
            weights = (alpha * scores).astype(BF16)
            seen = jnp.where(alpha > 0.0, 1.0, 0.0).astype(BF16)
            rhs = rhs + jnp.dot(seen, items, preferred_element_type=F32)
            image = image + jnp.dot(weights, items, preferred_element_type=F32)
    if last:
        image = image + jnp.dot(prev, high, preferred_element_type=F32)
        image = image + jnp.dot(prev, low, preferred_element_type=F32)
        pack((1.0 + conf_ref[...]) * rhs - image, msg_ref)
    elif closing:
        high = gram.astype(BF16)
        low = (gram - high.astype(F32)).astype(BF16)
        image = image + jnp.dot(prev, high, preferred_element_type=F32)
        image = image + jnp.dot(prev, low, preferred_element_type=F32)
        sums_ref[...] = (1.0 + conf_ref[...]) * rhs - image
    else:
        sums_ref[0] = rhs
        sums_ref[1] = image


def add_gram(gram, pieces, arrays, rows, info_ref, obs):
    me = info_ref[0]
    for (_, pair, offset, length), ref in zip(pieces, arrays):
        slot = lax.broadcasted_iota(jnp.int32, (length, gram.shape[0]), 0)
        slot = slot + (shard_index(me, pair) * rows + offset)
        for t in range(ref.shape[0]):
            tile_rows = ref[t]
            masked = jnp.where(slot < info_ref[1 + obs + t], tile_rows, jnp.zeros_like(tile_rows))
            gram = gram + lax.dot_general(
                masked, tile_rows, (((0,), (0,)), ((), ())), preferred_element_type=F32
            )
    return gram


def keep_kernel(in_ref, out_ref):
    for index in range(in_ref.shape[0]):
        out_ref[index] = in_ref[index]


def twin_kernel(pieces, rows, info_ref, twin_info_ref, alpha_ref, prev_ref, *refs):
    *arrays, part_ref = refs
    users, rank = prev_ref.shape
    obs = alpha_ref.shape[0]
    prev = prev_ref[...]
    gram = add_gram(jnp.zeros((rank, rank), F32), pieces, arrays, rows, info_ref, obs)
    rhs = jnp.zeros((users, rank), F32)
    image = jnp.zeros((users, rank), F32)
    conf = jnp.zeros((users, 1), F32)
    for p in range(obs):
        tile = twin_info_ref[1 + p]
        conf = jnp.maximum(conf, jnp.max(alpha_ref[p], axis=1, keepdims=True))
        for (spot, _, _, length), ref in zip(pieces, arrays):
            items = ref[tile]
            alpha = alpha_ref[p, :, spot : spot + length]
            scores = jnp.dot(prev, items.T, preferred_element_type=F32)
            weights = (alpha * scores).astype(BF16)
            seen = jnp.where(alpha > 0.0, 1.0, 0.0).astype(BF16)
            rhs = rhs + jnp.dot(seen, items, preferred_element_type=F32)
            image = image + jnp.dot(weights, items, preferred_element_type=F32)
    high = gram.astype(BF16)
    low = (gram - high.astype(F32)).astype(BF16)
    image = image + jnp.dot(prev, high, preferred_element_type=F32)
    image = image + jnp.dot(prev, low, preferred_element_type=F32)
    part_ref[...] = (1.0 + conf) * rhs - image


def join_kernel(mine_ref, part_ref, msg_ref):
    pack(mine_ref[...] + part_ref[...], msg_ref)


def collect_kernel(pieces, rows, info_ref, gram_ref, *refs):
    arrays = refs[: len(pieces)]
    picked_ref, turned_ref, high_ref, low_ref = refs[len(pieces) :]
    obs = picked_ref.shape[0]
    for p in range(obs):
        tile = info_ref[1 + p]
        for (spot, _, _, length), ref in zip(pieces, arrays):
            picked_ref[p, spot : spot + length, :] = ref[tile]
        for block in blocks(picked_ref.shape[1]):
            turned_ref[p, :, block] = picked_ref[p, block, :].T
    gram = add_gram(gram_ref[...], pieces, arrays, rows, info_ref, obs)
    high = gram.astype(BF16)
    high_ref[...] = high
    low_ref[...] = (gram - high.astype(F32)).astype(BF16)


def in_order(refs, order):
    return [refs[order.index(bits)] for bits in range(len(order))]


def round_kernel(step_index, order, n_stages, *refs):
    msgs = in_order(refs, order)
    refs = refs[len(order) :]
    prev_ref, high_ref, low_ref = refs[:3]
    alphas, picked, turned = (refs[3 + n * n_stages : 3 + (n + 1) * n_stages] for n in range(3))
    refs = refs[3 + 3 * n_stages :]
    summed = tree_sum([unpack(m) for m in msgs])
    if step_index == 0:
        (r_ref, msg_ref) = refs
        residual = summed - ridge_weight * prev_ref[...].astype(F32)
        direction = residual
        r_ref[...] = residual
    else:
        n_state = 1 if step_index == 1 else 3
        state = refs[:n_state]
        refs = refs[n_state:]
        if step_index == 1:
            residual = direction = state[0][...]
            solution = prev_ref[...].astype(F32)
        else:
            residual, direction, solution = (s[...] for s in state)
        image = summed + ridge_weight * direction
        norm_now = jnp.sum(residual * residual, axis=1, keepdims=True)
        step_size = norm_now / jnp.sum(direction * image, axis=1, keepdims=True)
        solution = solution + step_size * direction
        residual = residual - step_size * image
        norm_next = jnp.sum(residual * residual, axis=1, keepdims=True)
        direction = residual + (norm_next / norm_now) * direction
        if step_index < ITERS - 1:
            r_ref, d_ref, x_ref, msg_ref = refs
            r_ref[...] = residual
        else:
            n_ref, d_ref, x_ref, msg_ref = refs
            n_ref[...] = jnp.broadcast_to(norm_next, n_ref.shape)
        d_ref[...] = direction
        x_ref[...] = solution
    last = step_index == ITERS - 1
    rounded = direction.astype(BF16)
    users = direction.shape[0]
    both = jnp.concatenate([rounded, (direction - rounded.astype(F32)).astype(BF16)], axis=0)
    both = jnp.dot(both, high_ref[...], preferred_element_type=F32)
    image = both[:users] + both[users:] + jnp.dot(rounded, low_ref[...], preferred_element_type=F32)
    if last:
        total = jnp.sum(image * direction, axis=1, keepdims=True)
    for alpha_ref, ref, turned_ref in zip(alphas, picked, turned):
        for p in range(ref.shape[0]):
            for block in blocks(ref.shape[1]):
                items = ref[p, block, :]
                alpha = alpha_ref[p, :, block]
                scores = jnp.dot(rounded, turned_ref[p, :, block], preferred_element_type=F32)
                weights = (alpha * scores).astype(BF16)
                if last:
                    total = total + jnp.sum(weights.astype(F32) * scores, axis=1, keepdims=True)
                else:
                    image = image + jnp.dot(weights, items, preferred_element_type=F32)
    if last:
        msg_ref[...] = row_of(total, msg_ref.shape[0])
    else:
        pack(image, msg_ref)


def final_kernel(order, *refs):
    msgs = in_order(refs, order)
    n_ref, d_ref, x_ref, out_ref = refs[len(order) :]
    direction = d_ref[...]
    total = column_of(tree_sum([m[...] for m in msgs])[:1], 128)
    squares = jnp.sum(direction * direction, axis=1, keepdims=True)
    step_size = n_ref[...] / (total + ridge_weight * squares)
    for at in range(0, direction.shape[1], 128):
        out_ref[:, at : at + 128] = x_ref[:, at : at + 128] + step_size * direction[:, at : at + 128]


def permuted(array, axis, size, target):
    return lax.ppermute(array, axis, [(i, target(i)) for i in range(size)])


def tied(array, token):
    return lax.optimization_barrier((array, token))[0]


def gather_stages(own, size, plan, work, prepare, finish):
    send = functools.partial(permuted, axis="row", size=size)
    held = {0: own}
    bit = 8 if size >= 8 else 1
    while bit < size:
        held.update({s ^ bit: send(a, target=lambda i: i ^ bit) for s, a in held.items()})
        bit *= 2
    rows = own.shape[1]
    if size < 8:
        plan([[((s, s), 0, rows) for s in held]])
        work(list(held.values()))
        return

    def twin(array):
        return send(array, target=lambda i: i ^ 1)

    def first_way(array):
        return send(array, target=lambda i: i ^ (2 + 2 * (i & 1)))

    def second_way(array):
        return send(array, target=lambda i: i ^ (4 - 2 * (i & 1)))

    half = rows // 2
    whole, upper, lower = (0, rows), (0, half), (half, half)
    kinds = [
        [((0, 0), *whole), ((1, 1), *whole)],
        [((2, 4), *whole), ((5, 3), *upper), ((5, 3), *lower), ((4, 2), *whole), ((3, 5), *upper), ((3, 5), *lower)],
        [((6, 6), *whole)],
        [((7, 7), *whole)],
    ]
    early = plan([[((s ^ e, s ^ o), at, n) for s in held for (e, o), at, n in kind] for kind in kinds])

    one = [first_way(a) for a in held.values()]
    two = [second_way(tied(a, early)) for a in held.values()]
    token = work([x for a in held.values() for x in (a, twin(a))])
    ready = prepare(twin)
    one = [tied(a, (token, ready)) for a in one]
    two = [tied(a, token) for a in two]
    far = [second_way(a) for a in one]
    token = work([x for a, b in zip(one, two) for x in (a, twin(a[:, :half]), twin(a[:, half:]), b, twin(b[:, :half]), twin(b[:, half:]))])
    far = [tied(a, token) for a in far]
    finish(far, twin, ready)


def local(mesh, item_factors, tile_counts, observed_tiles, mask_words, confidence, previous):
    n_row, n_col = mesh.shape["row"], mesh.shape["col"]
    tiles, rows, rank = item_factors.shape
    users, obs, width = mask_words.shape
    slots = rows * n_row
    me = lax.axis_index("row").astype(jnp.int32).reshape(1)
    info = jnp.concatenate([me, observed_tiles[0], tile_counts])
    conf = confidence[:, None]
    words = jnp.transpose(mask_words, (1, 0, 2)).astype(BF16)
    shape = jax.ShapeDtypeStruct

    message = shape((users, rank), jnp.int16)
    vec = shape((users, rank), F32)
    sums = shape((2, users, rank), F32)
    gram_shape = shape((rank, rank), F32)
    stages, picked, turned, alphas, carry, scalars = [], [], [], [], [], []

    def masks_of(plan):
        for stage in plan:
            spot, pieces = 0, []
            for pair, offset, length in stage:
                pieces.append((spot, pair, offset, length))
                spot += length
            stages.append(pieces)
        sizes = [sum(length for _, _, _, length in pieces) for pieces in stages]
        *masks, kept_info = (
            call(
                functools.partial(masks_kernel, stages, rows),
                [shape((obs, users, size), F32) for size in sizes],
                (info, words, conf),
                1,
                2 * obs * users * sum(sizes) * width,
                "masks",
                [shape(info.shape, info.dtype)],
            )
        )
        alphas.extend(masks)
        scalars.append(kept_info)
        return alphas

    def work(arrays, closing=False):
        index = len(picked)
        first, last = index == 0, index == len(stages) - 1
        pieces, alpha = stages[index], alphas[index]
        size = alpha.shape[2]
        split = shape((rank, rank), BF16)
        kept, kept_turned, *carried = call(
            functools.partial(gather_kernel, pieces, rows, first, last, closing),
            [shape((obs, size, rank), BF16), shape((obs, rank, size), BF16)]
            + ([split, split, message] if last else [gram_shape, vec if closing else sums]),
            (*scalars, alpha, conf, previous, *arrays, *carry),
            1,
            2 * size * rank * (tiles * rank + 3 * obs * users),
            "stage",
        )
        carry[:] = carried
        picked.append(kept)
        turned.append(kept_turned)
        return carried, alphas

    def prepare(twin):
        (twin_info,) = call(keep_kernel, [], (twin(info),), 1, 0, "keep", [shape(info.shape, info.dtype)])
        return twin_info, twin(alphas[3]), twin(previous)

    def finish(far, twin, ready):
        pieces, alpha = stages[2], alphas[3]
        twin_info, twin_alpha, twin_prev = ready
        size = alpha.shape[2]
        flops = 2 * size * rank * (tiles * rank + 3 * obs * users)
        (part,) = call(
            functools.partial(twin_kernel, pieces, rows),
            [vec],
            (*scalars, twin_info, twin_alpha, twin_prev, *far),
            2,
            flops,
            "twin",
        )
        part = twin(part)
        gram, mine = work(far, True)[0]
        (msg,) = call(join_kernel, [message], (mine, part), 0, 0, "join")
        others = [twin(tied(a, msg)) for a in far]
        kept, kept_turned, high, low = call(
            functools.partial(collect_kernel, stages[3], rows),
            [shape((obs, size, rank), BF16), shape((obs, rank, size), BF16)] + [shape((rank, rank), BF16)] * 2,
            (*scalars, gram, *others),
            1,
            flops,
            "collect",
        )
        picked.append(kept)
        turned.append(kept_turned)
        carry[:] = high, low, msg

    gather_stages(item_factors, n_row, masks_of, work, prepare, finish)
    high, low, msg = carry

    order = [0, *range(2, n_col, 2), *range(1, n_col, 2)]

    def to_all(own):
        return [own] + [permuted(own, "col", n_col, lambda i: i ^ bits) for bits in order[1:]]

    state = []
    for index in range(ITERS):
        last = index == ITERS - 1
        msgs = to_all(msg)
        outs = [vec] if index == 0 else [vec, vec, vec]
        if last:
            outs = [shape((users, 128), F32), vec, vec]
        outs.append(shape((8, users), F32) if last else message)
        *state, msg = call(
            functools.partial(round_kernel, index, order, len(picked)),
            outs,
            (*msgs, previous, high, low, *alphas, *picked, *turned, *state),
            0,
            4 * obs * users * slots * rank,
            f"round{index}",
        )
    msgs = to_all(msg)
    (out,) = pl.pallas_call(
        functools.partial(final_kernel, order),
        out_shape=[vec],
        in_specs=[VMEM] * (n_col + 3),
        out_specs=[VMEM],
        compiler_params=pltpu.CompilerParams(vmem_limit_bytes=4 * 1024 * 1024),
        name="final",
    )(*msgs, *state)
    return out


def solution(mesh):
    return jax.shard_map(
        functools.partial(local, mesh),
        mesh=mesh,
        in_specs=(
            P("col", "row", None),
            P("col"),
            P("row", "col"),
            P("row", "col", None),
            P("row"),
            P("row", None),
        ),
        out_specs=P("row", None),
        check_vma=False,
    )
```

```python
import functools

import jax
import jax.numpy as jnp
from jax import lax
from jax.experimental import pallas as pl
from jax.experimental.pallas import tpu as pltpu
from jax.sharding import PartitionSpec as P

ITERS = 3
BLOCK = 256
ridge_weight = 0.1

SMEM = pl.BlockSpec(memory_space=pltpu.SMEM)
VMEM = pl.BlockSpec(memory_space=pltpu.VMEM)
F32 = jnp.float32
BF16 = jnp.bfloat16


def call(body, outs, args, n_smem, flops, name, scalars=()):
    kept = [pltpu.with_memory_space_constraint(a, pltpu.SMEM) for a in args[:n_smem]]
    return pl.pallas_call(
        body,
        out_shape=[pltpu.VMEM(o.shape, o.dtype) for o in outs] + [pltpu.SMEM(o.shape, o.dtype) for o in scalars],
        in_specs=[SMEM] * n_smem + [VMEM] * (len(args) - n_smem),
        out_specs=[VMEM] * len(outs) + [SMEM] * len(scalars),
        compiler_params=pltpu.CompilerParams(vmem_limit_bytes=24 * 1024 * 1024),
        cost_estimate=pl.CostEstimate(flops=flops, bytes_accessed=1 << 20, transcendentals=0),
        name=name,
    )(*kept, *args[n_smem:])


def column_of(row_values, lanes):
    return jnp.broadcast_to(row_values, (lanes, row_values.shape[1])).T


def row_of(column, rows):
    return jnp.broadcast_to(column, (column.shape[0], 128)).T[:rows]


def low_lanes(users):
    lane = lax.broadcasted_iota(jnp.int32, (users, 128), 1)
    return lane, lane < 8


def pack(values, out_ref):
    users, rank = values.shape
    top = jnp.max(jnp.abs(values), axis=1, keepdims=True)
    power = jnp.clip(jnp.ceil(jnp.log2(jnp.maximum(top, 1e-30))), -100.0, 127.0)
    scaled = jnp.round(values * jnp.exp2(15.0 - power))
    scaled = jnp.clip(scaled, -32767.0, 32767.0).astype(jnp.int32)
    lane, low = low_lanes(users)
    bit = jnp.right_shift(jnp.broadcast_to((power + 128.0).astype(jnp.int32), lane.shape), lane & 7) & 1
    head = scaled[:, :128]
    out_ref[:, :128] = jnp.where(low, (head & -2) | bit, head).astype(jnp.int16)
    out_ref[:, 128:] = scaled[:, 128:].astype(jnp.int16)


def unpack(ref):
    users = ref.shape[0]
    whole = ref[...].astype(jnp.int32)
    head = whole[:, :128]
    lane, low = low_lanes(users)
    bit = jnp.where(low, head & 1, 0)
    power = jnp.sum(jnp.left_shift(bit, lane & 7).astype(F32), axis=1, keepdims=True) - 128.0
    whole = jnp.concatenate([head - bit, whole[:, 128:]], axis=1)
    return whole.astype(F32) * jnp.exp2(power - 15.0)


def blocks(size):
    return [slice(at, min(at + BLOCK, size)) for at in range(0, size, BLOCK)]


def tree_sum(parts):
    while len(parts) > 1:
        parts = [parts[i] + parts[i + 1] for i in range(0, len(parts), 2)]
    return parts[0]


def shard_index(me, shards):
    even, odd = shards
    return me ^ (even + (me & 1) * (odd - even))


def masks_kernel(stages, rows, info_ref, words_ref, conf_ref, *out_refs):
    *out_refs, kept_ref = out_refs
    for index in range(info_ref.shape[0]):
        kept_ref[index] = info_ref[index]
    me = info_ref[0]
    obs, _, width = words_ref.shape
    for pieces, out_ref in zip(stages, out_refs):
        for block in blocks(out_ref.shape[2]):
            size = block.stop - block.start
            lane = lax.broadcasted_iota(jnp.int32, (1, size), 1)
            slot = jnp.zeros((1, size), jnp.int32)
            for spot, pair, offset, _ in pieces:
                place = spot - block.start
                if 0 <= place < size:
                    start = shard_index(me, pair) * rows + offset - place
                    slot = jnp.where(lane >= place, lane + start, slot)
            word_index = lax.broadcasted_iota(jnp.int32, (width, size), 0)
            spread = (word_index == jnp.right_shift(slot, 3)).astype(BF16)
            for p in range(obs):
                count = info_ref[1 + obs + info_ref[1 + p]]
                word = jnp.dot(words_ref[p], spread, preferred_element_type=F32).astype(jnp.int32)
                bits = jnp.right_shift(word, slot & 7) & 1
                bits = jnp.where(slot < count, bits, 0).astype(F32)
                out_ref[p, :, block] = bits * conf_ref[...]


def gather_kernel(pieces, rows, first, last, closing, *refs):
    info_ref, alpha_ref, conf_ref, prev_ref = refs[:4]
    at = 4
    arrays = refs[at : at + len(pieces)]
    at += len(pieces)
    if not first:
        gram_in, sums_in = refs[at : at + 2]
        at += 2
    picked_ref, turned_ref = refs[at : at + 2]
    at += 2
    if last:
        high_ref, low_ref, msg_ref = refs[at:]
    else:
        gram_ref, sums_ref = refs[at:]
    me = info_ref[0]
    users, rank = prev_ref.shape
    obs = alpha_ref.shape[0]
    tiles = arrays[0].shape[0]
    for p in range(obs):
        tile = info_ref[1 + p]
        for (spot, _, _, length), ref in zip(pieces, arrays):
            picked_ref[p, spot : spot + length, :] = ref[tile]
    gram = jnp.zeros((rank, rank), F32) if first else gram_in[...]
    for (_, pair, offset, length), ref in zip(pieces, arrays):
        slot = lax.broadcasted_iota(jnp.int32, (length, rank), 0)
        slot = slot + (shard_index(me, pair) * rows + offset)
        for t in range(tiles):
            tile_rows = ref[t]
            masked = jnp.where(slot < info_ref[1 + obs + t], tile_rows, jnp.zeros_like(tile_rows))
            gram = gram + lax.dot_general(
                masked, tile_rows, (((0,), (0,)), ((), ())), preferred_element_type=F32
            )
    if last:
        high = gram.astype(BF16)
        low = (gram - high.astype(F32)).astype(BF16)
        high_ref[...] = high
        low_ref[...] = low
    else:
        gram_ref[...] = gram
    prev = prev_ref[...]
    rhs = jnp.zeros((users, rank), F32) if first else sums_in[0]
    image = jnp.zeros((users, rank), F32) if first else sums_in[1]
    for p in range(obs):
        for block in blocks(picked_ref.shape[1]):
            items = picked_ref[p, block, :]
            turned = items.T
            turned_ref[p, :, block] = turned
            alpha = alpha_ref[p, :, block]
            scores = jnp.dot(prev, turned, preferred_element_type=F32)
            weights = (alpha * scores).astype(BF16)
            seen = jnp.where(alpha > 0.0, 1.0, 0.0).astype(BF16)
            rhs = rhs + jnp.dot(seen, items, preferred_element_type=F32)
            image = image + jnp.dot(weights, items, preferred_element_type=F32)
    if last:
        image = image + jnp.dot(prev, high, preferred_element_type=F32)
        image = image + jnp.dot(prev, low, preferred_element_type=F32)
        pack((1.0 + conf_ref[...]) * rhs - image, msg_ref)
    elif closing:
        high = gram.astype(BF16)
        low = (gram - high.astype(F32)).astype(BF16)
        image = image + jnp.dot(prev, high, preferred_element_type=F32)
        image = image + jnp.dot(prev, low, preferred_element_type=F32)
        sums_ref[...] = (1.0 + conf_ref[...]) * rhs - image
    else:
        sums_ref[0] = rhs
        sums_ref[1] = image


def add_gram(gram, pieces, arrays, rows, info_ref, obs):
    me = info_ref[0]
    for (_, pair, offset, length), ref in zip(pieces, arrays):
        slot = lax.broadcasted_iota(jnp.int32, (length, gram.shape[0]), 0)
        slot = slot + (shard_index(me, pair) * rows + offset)
        for t in range(ref.shape[0]):
            tile_rows = ref[t]
            masked = jnp.where(slot < info_ref[1 + obs + t], tile_rows, jnp.zeros_like(tile_rows))
            gram = gram + lax.dot_general(
                masked, tile_rows, (((0,), (0,)), ((), ())), preferred_element_type=F32
            )
    return gram


def keep_kernel(in_ref, out_ref):
    for index in range(in_ref.shape[0]):
        out_ref[index] = in_ref[index]


def twin_kernel(pieces, rows, info_ref, twin_info_ref, alpha_ref, prev_ref, *refs):
    *arrays, part_ref = refs
    users, rank = prev_ref.shape
    obs = alpha_ref.shape[0]
    prev = prev_ref[...]
    gram = add_gram(jnp.zeros((rank, rank), F32), pieces, arrays, rows, info_ref, obs)
    rhs = jnp.zeros((users, rank), F32)
    image = jnp.zeros((users, rank), F32)
    conf = jnp.zeros((users, 1), F32)
    for p in range(obs):
        tile = twin_info_ref[1 + p]
        conf = jnp.maximum(conf, jnp.max(alpha_ref[p], axis=1, keepdims=True))
        for (spot, _, _, length), ref in zip(pieces, arrays):
            items = ref[tile]
            alpha = alpha_ref[p, :, spot : spot + length]
            scores = jnp.dot(prev, items.T, preferred_element_type=F32)
            weights = (alpha * scores).astype(BF16)
            seen = jnp.where(alpha > 0.0, 1.0, 0.0).astype(BF16)
            rhs = rhs + jnp.dot(seen, items, preferred_element_type=F32)
            image = image + jnp.dot(weights, items, preferred_element_type=F32)
    high = gram.astype(BF16)
    low = (gram - high.astype(F32)).astype(BF16)
    image = image + jnp.dot(prev, high, preferred_element_type=F32)
    image = image + jnp.dot(prev, low, preferred_element_type=F32)
    part_ref[...] = (1.0 + conf) * rhs - image


def join_kernel(mine_ref, part_ref, msg_ref):
    pack(mine_ref[...] + part_ref[...], msg_ref)


def collect_kernel(pieces, rows, info_ref, gram_ref, *refs):
    arrays = refs[: len(pieces)]
    picked_ref, turned_ref, high_ref, low_ref = refs[len(pieces) :]
    obs = picked_ref.shape[0]
    for p in range(obs):
        tile = info_ref[1 + p]
        for (spot, _, _, length), ref in zip(pieces, arrays):
            picked_ref[p, spot : spot + length, :] = ref[tile]
        for block in blocks(picked_ref.shape[1]):
            turned_ref[p, :, block] = picked_ref[p, block, :].T
    gram = add_gram(gram_ref[...], pieces, arrays, rows, info_ref, obs)
    high = gram.astype(BF16)
    high_ref[...] = high
    low_ref[...] = (gram - high.astype(F32)).astype(BF16)


def in_order(refs, order):
    return [refs[order.index(bits)] for bits in range(len(order))]


def round_kernel(step_index, order, n_stages, *refs):
    msgs = in_order(refs, order)
    refs = refs[len(order) :]
    prev_ref, high_ref, low_ref = refs[:3]
    alphas, picked, turned = (refs[3 + n * n_stages : 3 + (n + 1) * n_stages] for n in range(3))
    refs = refs[3 + 3 * n_stages :]
    summed = tree_sum([unpack(m) for m in msgs])
    if step_index == 0:
        (r_ref, msg_ref) = refs
        residual = summed - ridge_weight * prev_ref[...].astype(F32)
        direction = residual
        r_ref[...] = residual
    else:
        n_state = 1 if step_index == 1 else 3
        state = refs[:n_state]
        refs = refs[n_state:]
        if step_index == 1:
            residual = direction = state[0][...]
            solution = prev_ref[...].astype(F32)
        else:
            residual, direction, solution = (s[...] for s in state)
        image = summed + ridge_weight * direction
        norm_now = jnp.sum(residual * residual, axis=1, keepdims=True)
        step_size = norm_now / jnp.sum(direction * image, axis=1, keepdims=True)
        solution = solution + step_size * direction
        residual = residual - step_size * image
        norm_next = jnp.sum(residual * residual, axis=1, keepdims=True)
        direction = residual + (norm_next / norm_now) * direction
        if step_index < ITERS - 1:
            r_ref, d_ref, x_ref, msg_ref = refs
            r_ref[...] = residual
        else:
            n_ref, d_ref, x_ref, msg_ref = refs
            n_ref[...] = jnp.broadcast_to(norm_next, n_ref.shape)
        d_ref[...] = direction
        x_ref[...] = solution
    last = step_index == ITERS - 1
    rounded = direction.astype(BF16)
    users = direction.shape[0]
    both = jnp.concatenate([rounded, (direction - rounded.astype(F32)).astype(BF16)], axis=0)
    both = jnp.dot(both, high_ref[...], preferred_element_type=F32)
    image = both[:users] + both[users:] + jnp.dot(rounded, low_ref[...], preferred_element_type=F32)
    if last:
        total = jnp.sum(image * direction, axis=1, keepdims=True)
    for alpha_ref, ref, turned_ref in zip(alphas, picked, turned):
        for p in range(ref.shape[0]):
            for block in blocks(ref.shape[1]):
                items = ref[p, block, :]
                alpha = alpha_ref[p, :, block]
                scores = jnp.dot(rounded, turned_ref[p, :, block], preferred_element_type=F32)
                weights = (alpha * scores).astype(BF16)
                if last:
                    total = total + jnp.sum(weights.astype(F32) * scores, axis=1, keepdims=True)
                else:
                    image = image + jnp.dot(weights, items, preferred_element_type=F32)
    if last:
        msg_ref[...] = row_of(total, msg_ref.shape[0])
    else:
        pack(image, msg_ref)


def final_kernel(order, *refs):
    msgs = in_order(refs, order)
    n_ref, d_ref, x_ref, out_ref = refs[len(order) :]
    direction = d_ref[...]
    total = column_of(tree_sum([m[...] for m in msgs])[:1], 128)
    squares = jnp.sum(direction * direction, axis=1, keepdims=True)
    step_size = n_ref[...] / (total + ridge_weight * squares)
    for at in range(0, direction.shape[1], 128):
        out_ref[:, at : at + 128] = x_ref[:, at : at + 128] + step_size * direction[:, at : at + 128]


def permuted(array, axis, size, target):
    return lax.ppermute(array, axis, [(i, target(i)) for i in range(size)])


def tied(array, token):
    return lax.optimization_barrier((array, token))[0]


def gather_stages(own, size, plan, work, prepare, finish):
    send = functools.partial(permuted, axis="row", size=size)
    held = {0: own}
    bit = 8 if size >= 8 else 1
    while bit < size:
        held.update({s ^ bit: send(a, target=lambda i: i ^ bit) for s, a in held.items()})
        bit *= 2
    rows = own.shape[1]
    if size < 8:
        plan([[((s, s), 0, rows) for s in held]])
        work(list(held.values()))
        return

    def twin(array):
        return send(array, target=lambda i: i ^ 1)

    def first_way(array):
        return send(array, target=lambda i: i ^ (2 + 2 * (i & 1)))

    def second_way(array):
        return send(array, target=lambda i: i ^ (4 - 2 * (i & 1)))

    half = rows // 2
    whole, upper, lower = (0, rows), (0, half), (half, half)
    kinds = [
        [((0, 0), *whole), ((1, 1), *whole)],
        [((2, 4), *whole), ((5, 3), *upper), ((5, 3), *lower), ((4, 2), *whole), ((3, 5), *upper), ((3, 5), *lower)],
        [((6, 6), *whole)],
        [((7, 7), *whole)],
    ]
    early = plan([[((s ^ e, s ^ o), at, n) for s in held for (e, o), at, n in kind] for kind in kinds])

    one = [first_way(a) for a in held.values()]
    two = [second_way(tied(a, early)) for a in held.values()]
    token = work([x for a in held.values() for x in (a, twin(a))])
    ready = prepare(twin)
    one = [tied(a, (token, ready)) for a in one]
    two = [tied(a, token) for a in two]
    far = [second_way(a) for a in one]
    token = work([x for a, b in zip(one, two) for x in (a, twin(a[:, :half]), twin(a[:, half:]), b, twin(b[:, :half]), twin(b[:, half:]))])
    far = [tied(a, token) for a in far]
    finish(far, twin, ready)


def local(mesh, item_factors, tile_counts, observed_tiles, mask_words, confidence, previous):
    n_row, n_col = mesh.shape["row"], mesh.shape["col"]
    tiles, rows, rank = item_factors.shape
    users, obs, width = mask_words.shape
    slots = rows * n_row
    me = lax.axis_index("row").astype(jnp.int32).reshape(1)
    info = jnp.concatenate([me, observed_tiles[0], tile_counts])
    conf = confidence[:, None]
    words = jnp.transpose(mask_words, (1, 0, 2)).astype(BF16)
    shape = jax.ShapeDtypeStruct

    message = shape((users, rank), jnp.int16)
    vec = shape((users, rank), F32)
    sums = shape((2, users, rank), F32)
    gram_shape = shape((rank, rank), F32)
    stages, picked, turned, alphas, carry, scalars = [], [], [], [], [], []

    def masks_of(plan):
        for stage in plan:
            spot, pieces = 0, []
            for pair, offset, length in stage:
                pieces.append((spot, pair, offset, length))
                spot += length
            stages.append(pieces)
        sizes = [sum(length for _, _, _, length in pieces) for pieces in stages]
        *masks, kept_info = (
            call(
                functools.partial(masks_kernel, stages, rows),
                [shape((obs, users, size), F32) for size in sizes],
                (info, words, conf),
                1,
                2 * obs * users * sum(sizes) * width,
                "masks",
                [shape(info.shape, info.dtype)],
            )
        )
        alphas.extend(masks)
        scalars.append(kept_info)
        return alphas

    def work(arrays, closing=False):
        index = len(picked)
        first, last = index == 0, index == len(stages) - 1
        pieces, alpha = stages[index], alphas[index]
        size = alpha.shape[2]
        split = shape((rank, rank), BF16)
        kept, kept_turned, *carried = call(
            functools.partial(gather_kernel, pieces, rows, first, last, closing),
            [shape((obs, size, rank), BF16), shape((obs, rank, size), BF16)]
            + ([split, split, message] if last else [gram_shape, vec if closing else sums]),
            (*scalars, alpha, conf, previous, *arrays, *carry),
            1,
            2 * size * rank * (tiles * rank + 3 * obs * users),
            "stage",
        )
        carry[:] = carried
        picked.append(kept)
        turned.append(kept_turned)
        return carried, alphas

    def prepare(twin):
        (twin_info,) = call(keep_kernel, [], (twin(info),), 1, 0, "keep", [shape(info.shape, info.dtype)])
        return twin_info, twin(alphas[3]), twin(previous)

    def finish(far, twin, ready):
        pieces, alpha = stages[2], alphas[3]
        twin_info, twin_alpha, twin_prev = ready
        size = alpha.shape[2]
        flops = 2 * size * rank * (tiles * rank + 3 * obs * users)
        (part,) = call(
            functools.partial(twin_kernel, pieces, rows),
            [vec],
            (*scalars, twin_info, twin_alpha, twin_prev, *far),
            2,
            flops,
            "twin",
        )
        part = twin(part)
        gram, mine = work(far, True)[0]
        (msg,) = call(join_kernel, [message], (mine, part), 0, 0, "join")
        others = [twin(tied(a, msg)) for a in far]
        kept, kept_turned, high, low = call(
            functools.partial(collect_kernel, stages[3], rows),
            [shape((obs, size, rank), BF16), shape((obs, rank, size), BF16)] + [shape((rank, rank), BF16)] * 2,
            (*scalars, gram, *others),
            1,
            flops,
            "collect",
        )
        picked.append(kept)
        turned.append(kept_turned)
        carry[:] = high, low, msg

    gather_stages(item_factors, n_row, masks_of, work, prepare, finish)
    high, low, msg = carry

    order = [0, *range(2, n_col, 2), *range(1, n_col, 2)]

    def partner(place, bits):
        row, col = place // n_col, place % n_col
        if row & 1 and n_col > 2:
            bits = (bits & ~3) | (0, 2, 1, 3)[bits & 3]
        return row * n_col + (col ^ bits)

    def sent(own, bits):
        return lax.ppermute(own, ("row", "col"), [(i, partner(i, bits)) for i in range(n_row * n_col)])

    def to_all(own):
        return [own] + [sent(own, bits) for bits in order[1:]]

    state = []
    for index in range(ITERS):
        last = index == ITERS - 1
        msgs = to_all(msg)
        outs = [vec] if index == 0 else [vec, vec, vec]
        if last:
            outs = [shape((users, 128), F32), vec, vec]
        outs.append(shape((8, users), F32) if last else message)
        *state, msg = call(
            functools.partial(round_kernel, index, order, len(picked)),
            outs,
            (*msgs, previous, high, low, *alphas, *picked, *turned, *state),
            0,
            4 * obs * users * slots * rank,
            f"round{index}",
        )
    msgs = to_all(msg)
    (out,) = pl.pallas_call(
        functools.partial(final_kernel, order),
        out_shape=[vec],
        in_specs=[VMEM] * (n_col + 3),
        out_specs=[VMEM],
        compiler_params=pltpu.CompilerParams(vmem_limit_bytes=4 * 1024 * 1024),
        name="final",
    )(*msgs, *state)
    return out


def solution(mesh):
    return jax.shard_map(
        functools.partial(local, mesh),
        mesh=mesh,
        in_specs=(
            P("col", "row", None),
            P("col"),
            P("row", "col"),
            P("row", "col", None),
            P("row"),
            P("row", None),
        ),
        out_specs=P("row", None),
        check_vma=False,
    )
```

```python
import functools

import jax
import jax.numpy as jnp
from jax import lax
from jax.experimental import pallas as pl
from jax.experimental.pallas import tpu as pltpu
from jax.sharding import PartitionSpec as P

ITERS = 3
BLOCK = 256
ridge_weight = 0.1

SMEM = pl.BlockSpec(memory_space=pltpu.SMEM)
VMEM = pl.BlockSpec(memory_space=pltpu.VMEM)
F32 = jnp.float32
BF16 = jnp.bfloat16


def call(body, outs, args, n_smem, flops, name, scalars=()):
    kept = [pltpu.with_memory_space_constraint(a, pltpu.SMEM) for a in args[:n_smem]]
    return pl.pallas_call(
        body,
        out_shape=[pltpu.VMEM(o.shape, o.dtype) for o in outs] + [pltpu.SMEM(o.shape, o.dtype) for o in scalars],
        in_specs=[SMEM] * n_smem + [VMEM] * (len(args) - n_smem),
        out_specs=[VMEM] * len(outs) + [SMEM] * len(scalars),
        compiler_params=pltpu.CompilerParams(vmem_limit_bytes=24 * 1024 * 1024),
        cost_estimate=pl.CostEstimate(flops=flops, bytes_accessed=1 << 20, transcendentals=0),
        name=name,
    )(*kept, *args[n_smem:])


def column_of(row_values, lanes):
    return jnp.broadcast_to(row_values, (lanes, row_values.shape[1])).T


def row_of(column, rows):
    return jnp.broadcast_to(column, (column.shape[0], 128)).T[:rows]


def low_lanes(users):
    lane = lax.broadcasted_iota(jnp.int32, (users, 128), 1)
    return lane, lane < 8


def pack(values, out_ref):
    users, rank = values.shape
    top = jnp.max(jnp.abs(values), axis=1, keepdims=True)
    power = jnp.clip(jnp.ceil(jnp.log2(jnp.maximum(top, 1e-30))), -100.0, 127.0)
    scaled = jnp.round(values * jnp.exp2(15.0 - power))
    scaled = jnp.clip(scaled, -32767.0, 32767.0).astype(jnp.int32)
    lane, low = low_lanes(users)
    bit = jnp.right_shift(jnp.broadcast_to((power + 128.0).astype(jnp.int32), lane.shape), lane & 7) & 1
    head = scaled[:, :128]
    out_ref[:, :128] = jnp.where(low, (head & -2) | bit, head).astype(jnp.int16)
    out_ref[:, 128:] = scaled[:, 128:].astype(jnp.int16)


def unpack(ref):
    users = ref.shape[0]
    whole = ref[...].astype(jnp.int32)
    head = whole[:, :128]
    lane, low = low_lanes(users)
    bit = jnp.where(low, head & 1, 0)
    power = jnp.sum(jnp.left_shift(bit, lane & 7).astype(F32), axis=1, keepdims=True) - 128.0
    whole = jnp.concatenate([head - bit, whole[:, 128:]], axis=1)
    return whole.astype(F32) * jnp.exp2(power - 15.0)


def blocks(size):
    return [slice(at, min(at + BLOCK, size)) for at in range(0, size, BLOCK)]


def tree_sum(parts):
    while len(parts) > 1:
        parts = [parts[i] + parts[i + 1] for i in range(0, len(parts), 2)]
    return parts[0]


def shard_index(me, shards):
    even, odd = shards
    return me ^ (even + (me & 1) * (odd - even))


def masks_kernel(stages, rows, info_ref, words_ref, conf_ref, *out_refs):
    *out_refs, kept_ref = out_refs
    for index in range(info_ref.shape[0]):
        kept_ref[index] = info_ref[index]
    me = info_ref[0]
    obs, _, width = words_ref.shape
    for pieces, out_ref in zip(stages, out_refs):
        for block in blocks(out_ref.shape[2]):
            size = block.stop - block.start
            lane = lax.broadcasted_iota(jnp.int32, (1, size), 1)
            slot = jnp.zeros((1, size), jnp.int32)
            for spot, pair, offset, _ in pieces:
                place = spot - block.start
                if 0 <= place < size:
                    start = shard_index(me, pair) * rows + offset - place
                    slot = jnp.where(lane >= place, lane + start, slot)
            word_index = lax.broadcasted_iota(jnp.int32, (width, size), 0)
            spread = (word_index == jnp.right_shift(slot, 3)).astype(BF16)
            for p in range(obs):
                count = info_ref[1 + obs + info_ref[1 + p]]
                word = jnp.dot(words_ref[p], spread, preferred_element_type=F32).astype(jnp.int32)
                bits = jnp.right_shift(word, slot & 7) & 1
                bits = jnp.where(slot < count, bits, 0).astype(F32)
                out_ref[p, :, block] = bits * conf_ref[...]


def gather_kernel(pieces, rows, first, last, closing, *refs):
    info_ref, alpha_ref, conf_ref, prev_ref = refs[:4]
    at = 4
    arrays = refs[at : at + len(pieces)]
    at += len(pieces)
    if not first:
        gram_in, sums_in = refs[at : at + 2]
        at += 2
    picked_ref, turned_ref = refs[at : at + 2]
    at += 2
    if last:
        high_ref, low_ref, msg_ref = refs[at:]
    else:
        gram_ref, sums_ref = refs[at:]
    me = info_ref[0]
    users, rank = prev_ref.shape
    obs = alpha_ref.shape[0]
    tiles = arrays[0].shape[0]
    for p in range(obs):
        tile = info_ref[1 + p]
        for (spot, _, _, length), ref in zip(pieces, arrays):
            picked_ref[p, spot : spot + length, :] = ref[tile]
    gram = jnp.zeros((rank, rank), F32) if first else gram_in[...]
    for (_, pair, offset, length), ref in zip(pieces, arrays):
        slot = lax.broadcasted_iota(jnp.int32, (length, rank), 0)
        slot = slot + (shard_index(me, pair) * rows + offset)
        for t in range(tiles):
            tile_rows = ref[t]
            masked = jnp.where(slot < info_ref[1 + obs + t], tile_rows, jnp.zeros_like(tile_rows))
            gram = gram + lax.dot_general(
                masked, tile_rows, (((0,), (0,)), ((), ())), preferred_element_type=F32
            )
    if last:
        high = gram.astype(BF16)
        low = (gram - high.astype(F32)).astype(BF16)
        high_ref[...] = high
        low_ref[...] = low
    else:
        gram_ref[...] = gram
    prev = prev_ref[...]
    rhs = jnp.zeros((users, rank), F32) if first else sums_in[0]
    image = jnp.zeros((users, rank), F32) if first else sums_in[1]
    for p in range(obs):
        for block in blocks(picked_ref.shape[1]):
            items = picked_ref[p, block, :]
            turned = items.T
            turned_ref[p, :, block] = turned
            alpha = alpha_ref[p, :, block]
            scores = jnp.dot(prev, turned, preferred_element_type=F32)
            weights = (alpha * scores).astype(BF16)
            seen = jnp.where(alpha > 0.0, 1.0, 0.0).astype(BF16)
            rhs = rhs + jnp.dot(seen, items, preferred_element_type=F32)
            image = image + jnp.dot(weights, items, preferred_element_type=F32)
    if last:
        image = image + jnp.dot(prev, high, preferred_element_type=F32)
        image = image + jnp.dot(prev, low, preferred_element_type=F32)
        pack((1.0 + conf_ref[...]) * rhs - image, msg_ref)
    elif closing:
        high = gram.astype(BF16)
        low = (gram - high.astype(F32)).astype(BF16)
        image = image + jnp.dot(prev, high, preferred_element_type=F32)
        image = image + jnp.dot(prev, low, preferred_element_type=F32)
        sums_ref[...] = (1.0 + conf_ref[...]) * rhs - image
    else:
        sums_ref[0] = rhs
        sums_ref[1] = image


def add_gram(gram, pieces, arrays, rows, info_ref, obs):
    me = info_ref[0]
    for (_, pair, offset, length), ref in zip(pieces, arrays):
        slot = lax.broadcasted_iota(jnp.int32, (length, gram.shape[0]), 0)
        slot = slot + (shard_index(me, pair) * rows + offset)
        for t in range(ref.shape[0]):
            tile_rows = ref[t]
            masked = jnp.where(slot < info_ref[1 + obs + t], tile_rows, jnp.zeros_like(tile_rows))
            gram = gram + lax.dot_general(
                masked, tile_rows, (((0,), (0,)), ((), ())), preferred_element_type=F32
            )
    return gram


def keep_kernel(in_ref, out_ref):
    for index in range(in_ref.shape[0]):
        out_ref[index] = in_ref[index]


def twin_kernel(pieces, rows, info_ref, twin_info_ref, alpha_ref, prev_ref, *refs):
    *arrays, part_ref = refs
    users, rank = prev_ref.shape
    obs = alpha_ref.shape[0]
    prev = prev_ref[...]
    gram = add_gram(jnp.zeros((rank, rank), F32), pieces, arrays, rows, info_ref, obs)
    rhs = jnp.zeros((users, rank), F32)
    image = jnp.zeros((users, rank), F32)
    conf = jnp.zeros((users, 1), F32)
    for p in range(obs):
        tile = twin_info_ref[1 + p]
        conf = jnp.maximum(conf, jnp.max(alpha_ref[p], axis=1, keepdims=True))
        for (spot, _, _, length), ref in zip(pieces, arrays):
            items = ref[tile]
            alpha = alpha_ref[p, :, spot : spot + length]
            scores = jnp.dot(prev, items.T, preferred_element_type=F32)
            weights = (alpha * scores).astype(BF16)
            seen = jnp.where(alpha > 0.0, 1.0, 0.0).astype(BF16)
            rhs = rhs + jnp.dot(seen, items, preferred_element_type=F32)
            image = image + jnp.dot(weights, items, preferred_element_type=F32)
    high = gram.astype(BF16)
    low = (gram - high.astype(F32)).astype(BF16)
    image = image + jnp.dot(prev, high, preferred_element_type=F32)
    image = image + jnp.dot(prev, low, preferred_element_type=F32)
    pack((1.0 + conf) * rhs - image, part_ref)


def join_kernel(mine_ref, part_ref, msg_ref):
    pack(mine_ref[...] + unpack(part_ref), msg_ref)


def collect_kernel(pieces, rows, info_ref, gram_ref, *refs):
    arrays = refs[: len(pieces)]
    picked_ref, turned_ref, high_ref, low_ref = refs[len(pieces) :]
    obs = picked_ref.shape[0]
    for p in range(obs):
        tile = info_ref[1 + p]
        for (spot, _, _, length), ref in zip(pieces, arrays):
            picked_ref[p, spot : spot + length, :] = ref[tile]
        for block in blocks(picked_ref.shape[1]):
            turned_ref[p, :, block] = picked_ref[p, block, :].T
    gram = add_gram(gram_ref[...], pieces, arrays, rows, info_ref, obs)
    high = gram.astype(BF16)
    high_ref[...] = high
    low_ref[...] = (gram - high.astype(F32)).astype(BF16)


def in_order(refs, order):
    return [refs[order.index(bits)] for bits in range(len(order))]


def round_kernel(step_index, order, n_stages, *refs):
    msgs = in_order(refs, order)
    refs = refs[len(order) :]
    prev_ref, high_ref, low_ref = refs[:3]
    alphas, picked, turned = (refs[3 + n * n_stages : 3 + (n + 1) * n_stages] for n in range(3))
    refs = refs[3 + 3 * n_stages :]
    summed = tree_sum([unpack(m) for m in msgs])
    if step_index == 0:
        (r_ref, msg_ref) = refs
        residual = summed - ridge_weight * prev_ref[...].astype(F32)
        direction = residual
        r_ref[...] = residual
    else:
        n_state = 1 if step_index == 1 else 3
        state = refs[:n_state]
        refs = refs[n_state:]
        if step_index == 1:
            residual = direction = state[0][...]
            solution = prev_ref[...].astype(F32)
        else:
            residual, direction, solution = (s[...] for s in state)
        image = summed + ridge_weight * direction
        norm_now = jnp.sum(residual * residual, axis=1, keepdims=True)
        step_size = norm_now / jnp.sum(direction * image, axis=1, keepdims=True)
        solution = solution + step_size * direction
        residual = residual - step_size * image
        norm_next = jnp.sum(residual * residual, axis=1, keepdims=True)
        direction = residual + (norm_next / norm_now) * direction
        if step_index < ITERS - 1:
            r_ref, d_ref, x_ref, msg_ref = refs
            r_ref[...] = residual
        else:
            n_ref, d_ref, x_ref, msg_ref = refs
            n_ref[...] = jnp.broadcast_to(norm_next, n_ref.shape)
        d_ref[...] = direction
        x_ref[...] = solution
    last = step_index == ITERS - 1
    rounded = direction.astype(BF16)
    users = direction.shape[0]
    both = jnp.concatenate([rounded, (direction - rounded.astype(F32)).astype(BF16)], axis=0)
    both = jnp.dot(both, high_ref[...], preferred_element_type=F32)
    image = both[:users] + both[users:] + jnp.dot(rounded, low_ref[...], preferred_element_type=F32)
    if last:
        total = jnp.sum(image * direction, axis=1, keepdims=True)
    for alpha_ref, ref, turned_ref in zip(alphas, picked, turned):
        for p in range(ref.shape[0]):
            for block in blocks(ref.shape[1]):
                items = ref[p, block, :]
                alpha = alpha_ref[p, :, block]
                scores = jnp.dot(rounded, turned_ref[p, :, block], preferred_element_type=F32)
                weights = (alpha * scores).astype(BF16)
                if last:
                    total = total + jnp.sum(weights.astype(F32) * scores, axis=1, keepdims=True)
                else:
                    image = image + jnp.dot(weights, items, preferred_element_type=F32)
    if last:
        msg_ref[...] = row_of(total, msg_ref.shape[0])
    else:
        pack(image, msg_ref)


def final_kernel(order, *refs):
    msgs = in_order(refs, order)
    n_ref, d_ref, x_ref, out_ref = refs[len(order) :]
    direction = d_ref[...]
    total = column_of(tree_sum([m[...] for m in msgs])[:1], 128)
    squares = jnp.sum(direction * direction, axis=1, keepdims=True)
    step_size = n_ref[...] / (total + ridge_weight * squares)
    for at in range(0, direction.shape[1], 128):
        out_ref[:, at : at + 128] = x_ref[:, at : at + 128] + step_size * direction[:, at : at + 128]


def permuted(array, axis, size, target):
    return lax.ppermute(array, axis, [(i, target(i)) for i in range(size)])


def tied(array, token):
    return lax.optimization_barrier((array, token))[0]


def gather_stages(own, size, plan, work, prepare, finish):
    send = functools.partial(permuted, axis="row", size=size)
    held = {0: own}
    bit = 8 if size >= 8 else 1
    while bit < size:
        held.update({s ^ bit: send(a, target=lambda i: i ^ bit) for s, a in held.items()})
        bit *= 2
    rows = own.shape[1]
    if size < 8:
        plan([[((s, s), 0, rows) for s in held]])
        work(list(held.values()))
        return

    def twin(array):
        return send(array, target=lambda i: i ^ 1)

    def first_way(array):
        return send(array, target=lambda i: i ^ (2 + 2 * (i & 1)))

    def second_way(array):
        return send(array, target=lambda i: i ^ (4 - 2 * (i & 1)))

    half = rows // 2
    whole, upper, lower = (0, rows), (0, half), (half, half)
    kinds = [
        [((0, 0), *whole), ((1, 1), *whole)],
        [((2, 4), *whole), ((5, 3), *upper), ((5, 3), *lower), ((4, 2), *whole), ((3, 5), *upper), ((3, 5), *lower)],
        [((6, 6), *whole)],
        [((7, 7), *whole)],
    ]
    early = plan([[((s ^ e, s ^ o), at, n) for s in held for (e, o), at, n in kind] for kind in kinds])

    one = [first_way(a) for a in held.values()]
    two = [second_way(tied(a, early)) for a in held.values()]
    token = work([x for a in held.values() for x in (a, twin(a))])
    ready = prepare(twin)
    one = [tied(a, (token, ready)) for a in one]
    two = [tied(a, token) for a in two]
    far = [second_way(a) for a in one]
    token = work([x for a, b in zip(one, two) for x in (a, twin(a[:, :half]), twin(a[:, half:]), b, twin(b[:, :half]), twin(b[:, half:]))])
    far = [tied(a, token) for a in far]
    finish(far, twin, ready)


def local(mesh, item_factors, tile_counts, observed_tiles, mask_words, confidence, previous):
    n_row, n_col = mesh.shape["row"], mesh.shape["col"]
    tiles, rows, rank = item_factors.shape
    users, obs, width = mask_words.shape
    slots = rows * n_row
    me = lax.axis_index("row").astype(jnp.int32).reshape(1)
    info = jnp.concatenate([me, observed_tiles[0], tile_counts])
    conf = confidence[:, None]
    words = jnp.transpose(mask_words, (1, 0, 2)).astype(BF16)
    shape = jax.ShapeDtypeStruct

    message = shape((users, rank), jnp.int16)
    vec = shape((users, rank), F32)
    sums = shape((2, users, rank), F32)
    gram_shape = shape((rank, rank), F32)
    stages, picked, turned, alphas, carry, scalars = [], [], [], [], [], []

    def masks_of(plan):
        for stage in plan:
            spot, pieces = 0, []
            for pair, offset, length in stage:
                pieces.append((spot, pair, offset, length))
                spot += length
            stages.append(pieces)
        sizes = [sum(length for _, _, _, length in pieces) for pieces in stages]
        *masks, kept_info = (
            call(
                functools.partial(masks_kernel, stages, rows),
                [shape((obs, users, size), F32) for size in sizes],
                (info, words, conf),
                1,
                2 * obs * users * sum(sizes) * width,
                "masks",
                [shape(info.shape, info.dtype)],
            )
        )
        alphas.extend(masks)
        scalars.append(kept_info)
        return alphas

    def work(arrays, closing=False):
        index = len(picked)
        first, last = index == 0, index == len(stages) - 1
        pieces, alpha = stages[index], alphas[index]
        size = alpha.shape[2]
        split = shape((rank, rank), BF16)
        kept, kept_turned, *carried = call(
            functools.partial(gather_kernel, pieces, rows, first, last, closing),
            [shape((obs, size, rank), BF16), shape((obs, rank, size), BF16)]
            + ([split, split, message] if last else [gram_shape, vec if closing else sums]),
            (*scalars, alpha, conf, previous, *arrays, *carry),
            1,
            2 * size * rank * (tiles * rank + 3 * obs * users),
            "stage",
        )
        carry[:] = carried
        picked.append(kept)
        turned.append(kept_turned)
        return carried, alphas

    def prepare(twin):
        (twin_info,) = call(keep_kernel, [], (twin(info),), 1, 0, "keep", [shape(info.shape, info.dtype)])
        return twin_info, twin(alphas[3]), twin(previous)

    def finish(far, twin, ready):
        pieces, alpha = stages[2], alphas[3]
        twin_info, twin_alpha, twin_prev = ready
        size = alpha.shape[2]
        flops = 2 * size * rank * (tiles * rank + 3 * obs * users)
        (part,) = call(
            functools.partial(twin_kernel, pieces, rows),
            [message],
            (*scalars, twin_info, twin_alpha, twin_prev, *far),
            2,
            flops,
            "twin",
        )
        part = twin(part)
        gram, mine = work(far, True)[0]
        (msg,) = call(join_kernel, [message], (mine, part), 0, 0, "join")
        others = [twin(tied(a, msg)) for a in far]
        kept, kept_turned, high, low = call(
            functools.partial(collect_kernel, stages[3], rows),
            [shape((obs, size, rank), BF16), shape((obs, rank, size), BF16)] + [shape((rank, rank), BF16)] * 2,
            (*scalars, gram, *others),
            1,
            flops,
            "collect",
        )
        picked.append(kept)
        turned.append(kept_turned)
        carry[:] = high, low, msg

    gather_stages(item_factors, n_row, masks_of, work, prepare, finish)
    high, low, msg = carry

    order = [0, *range(2, n_col, 2), *range(1, n_col, 2)]

    def partner(place, bits):
        row, col = place // n_col, place % n_col
        if row & 1 and n_col > 2:
            bits = (bits & ~3) | (0, 2, 1, 3)[bits & 3]
        return row * n_col + (col ^ bits)

    def sent(own, bits):
        return lax.ppermute(own, ("row", "col"), [(i, partner(i, bits)) for i in range(n_row * n_col)])

    def to_all(own):
        return [own] + [sent(own, bits) for bits in order[1:]]

    state = []
    for index in range(ITERS):
        last = index == ITERS - 1
        msgs = to_all(msg)
        outs = [vec] if index == 0 else [vec, vec, vec]
        if last:
            outs = [shape((users, 128), F32), vec, vec]
        outs.append(shape((8, users), F32) if last else message)
        *state, msg = call(
            functools.partial(round_kernel, index, order, len(picked)),
            outs,
            (*msgs, previous, high, low, *alphas, *picked, *turned, *state),
            0,
            4 * obs * users * slots * rank,
            f"round{index}",
        )
    msgs = to_all(msg)
    (out,) = pl.pallas_call(
        functools.partial(final_kernel, order),
        out_shape=[vec],
        in_specs=[VMEM] * (n_col + 3),
        out_specs=[VMEM],
        compiler_params=pltpu.CompilerParams(vmem_limit_bytes=4 * 1024 * 1024),
        name="final",
    )(*msgs, *state)
    return out


def solution(mesh):
    return jax.shard_map(
        functools.partial(local, mesh),
        mesh=mesh,
        in_specs=(
            P("col", "row", None),
            P("col"),
            P("row", "col"),
            P("row", "col", None),
            P("row"),
            P("row", None),
        ),
        out_specs=P("row", None),
        check_vma=False,
    )
```

```python
import functools

import jax
import jax.numpy as jnp
from jax import lax
from jax.experimental import pallas as pl
from jax.experimental.pallas import tpu as pltpu
from jax.sharding import PartitionSpec as P

ITERS = 3
BLOCK = 256
ridge_weight = 0.1

SMEM = pl.BlockSpec(memory_space=pltpu.SMEM)
VMEM = pl.BlockSpec(memory_space=pltpu.VMEM)
F32 = jnp.float32
BF16 = jnp.bfloat16


def call(body, outs, args, n_smem, flops, name, scalars=()):
    kept = [pltpu.with_memory_space_constraint(a, pltpu.SMEM) for a in args[:n_smem]]
    return pl.pallas_call(
        body,
        out_shape=[pltpu.VMEM(o.shape, o.dtype) for o in outs] + [pltpu.SMEM(o.shape, o.dtype) for o in scalars],
        in_specs=[SMEM] * n_smem + [VMEM] * (len(args) - n_smem),
        out_specs=[VMEM] * len(outs) + [SMEM] * len(scalars),
        compiler_params=pltpu.CompilerParams(vmem_limit_bytes=24 * 1024 * 1024),
        cost_estimate=pl.CostEstimate(flops=flops, bytes_accessed=1 << 20, transcendentals=0),
        name=name,
    )(*kept, *args[n_smem:])


def column_of(row_values, lanes):
    return jnp.broadcast_to(row_values, (lanes, row_values.shape[1])).T


def row_of(column, rows):
    return jnp.broadcast_to(column, (column.shape[0], 128)).T[:rows]


def low_lanes(users):
    lane = lax.broadcasted_iota(jnp.int32, (users, 128), 1)
    return lane, lane < 8


def pack(values, out_ref):
    users, rank = values.shape
    top = jnp.max(jnp.abs(values), axis=1, keepdims=True)
    power = jnp.clip(jnp.ceil(jnp.log2(jnp.maximum(top, 1e-30))), -100.0, 127.0)
    scaled = jnp.round(values * jnp.exp2(15.0 - power))
    scaled = jnp.clip(scaled, -32767.0, 32767.0).astype(jnp.int32)
    lane, low = low_lanes(users)
    bit = jnp.right_shift(jnp.broadcast_to((power + 128.0).astype(jnp.int32), lane.shape), lane & 7) & 1
    head = scaled[:, :128]
    out_ref[:, :128] = jnp.where(low, (head & -2) | bit, head).astype(jnp.int16)
    out_ref[:, 128:] = scaled[:, 128:].astype(jnp.int16)


def unpack(ref):
    users = ref.shape[0]
    whole = ref[...].astype(jnp.int32)
    head = whole[:, :128]
    lane, low = low_lanes(users)
    bit = jnp.where(low, head & 1, 0)
    power = jnp.sum(jnp.left_shift(bit, lane & 7).astype(F32), axis=1, keepdims=True) - 128.0
    whole = jnp.concatenate([head - bit, whole[:, 128:]], axis=1)
    return whole.astype(F32) * jnp.exp2(power - 15.0)


def blocks(size):
    return [slice(at, min(at + BLOCK, size)) for at in range(0, size, BLOCK)]


def tree_sum(parts):
    while len(parts) > 1:
        parts = [parts[i] + parts[i + 1] for i in range(0, len(parts), 2)]
    return parts[0]


def shard_index(me, shards):
    even, odd = shards
    return me ^ (even + (me & 1) * (odd - even))


def masks_kernel(stages, rows, info_ref, words_ref, conf_ref, *out_refs):
    *out_refs, kept_ref = out_refs
    for index in range(info_ref.shape[0]):
        kept_ref[index] = info_ref[index]
    me = info_ref[0]
    obs, _, width = words_ref.shape
    for pieces, out_ref in zip(stages, out_refs):
        for block in blocks(out_ref.shape[2]):
            size = block.stop - block.start
            lane = lax.broadcasted_iota(jnp.int32, (1, size), 1)
            slot = jnp.zeros((1, size), jnp.int32)
            for spot, pair, offset, _ in pieces:
                place = spot - block.start
                if 0 <= place < size:
                    start = shard_index(me, pair) * rows + offset - place
                    slot = jnp.where(lane >= place, lane + start, slot)
            word_index = lax.broadcasted_iota(jnp.int32, (width, size), 0)
            spread = (word_index == jnp.right_shift(slot, 3)).astype(BF16)
            for p in range(obs):
                count = info_ref[1 + obs + info_ref[1 + p]]
                word = jnp.dot(words_ref[p], spread, preferred_element_type=F32).astype(jnp.int32)
                bits = jnp.right_shift(word, slot & 7) & 1
                bits = jnp.where(slot < count, bits, 0).astype(F32)
                out_ref[p, :, block] = bits * conf_ref[...]


def gather_kernel(pieces, rows, first, last, closing, *refs):
    info_ref, alpha_ref, conf_ref, prev_ref = refs[:4]
    at = 4
    arrays = refs[at : at + len(pieces)]
    at += len(pieces)
    if not first:
        gram_in, sums_in = refs[at : at + 2]
        at += 2
    picked_ref, turned_ref = refs[at : at + 2]
    at += 2
    if last:
        high_ref, low_ref, msg_ref = refs[at:]
    else:
        gram_ref, sums_ref = refs[at:]
    me = info_ref[0]
    users, rank = prev_ref.shape
    obs = alpha_ref.shape[0]
    tiles = arrays[0].shape[0]
    for p in range(obs):
        tile = info_ref[1 + p]
        for (spot, _, _, length), ref in zip(pieces, arrays):
            picked_ref[p, spot : spot + length, :] = ref[tile]
    gram = jnp.zeros((rank, rank), F32) if first else gram_in[...]
    for (_, pair, offset, length), ref in zip(pieces, arrays):
        slot = lax.broadcasted_iota(jnp.int32, (length, rank), 0)
        slot = slot + (shard_index(me, pair) * rows + offset)
        for t in range(tiles):
            tile_rows = ref[t]
            masked = jnp.where(slot < info_ref[1 + obs + t], tile_rows, jnp.zeros_like(tile_rows))
            gram = gram + lax.dot_general(
                masked, tile_rows, (((0,), (0,)), ((), ())), preferred_element_type=F32
            )
    if last:
        high = gram.astype(BF16)
        low = (gram - high.astype(F32)).astype(BF16)
        high_ref[...] = high
        low_ref[...] = low
    else:
        gram_ref[...] = gram
    prev = prev_ref[...]
    rhs = jnp.zeros((users, rank), F32) if first else sums_in[0]
    image = jnp.zeros((users, rank), F32) if first else sums_in[1]
    for p in range(obs):
        for block in blocks(picked_ref.shape[1]):
            items = picked_ref[p, block, :]
            turned = items.T
            turned_ref[p, :, block] = turned
            alpha = alpha_ref[p, :, block]
            scores = jnp.dot(prev, turned, preferred_element_type=F32)
            weights = (alpha * scores).astype(BF16)
            seen = jnp.where(alpha > 0.0, 1.0, 0.0).astype(BF16)
            rhs = rhs + jnp.dot(seen, items, preferred_element_type=F32)
            image = image + jnp.dot(weights, items, preferred_element_type=F32)
    if last:
        image = image + jnp.dot(prev, high, preferred_element_type=F32)
        image = image + jnp.dot(prev, low, preferred_element_type=F32)
        pack((1.0 + conf_ref[...]) * rhs - image, msg_ref)
    elif closing:
        high = gram.astype(BF16)
        low = (gram - high.astype(F32)).astype(BF16)
        image = image + jnp.dot(prev, high, preferred_element_type=F32)
        image = image + jnp.dot(prev, low, preferred_element_type=F32)
        sums_ref[...] = (1.0 + conf_ref[...]) * rhs - image
    else:
        sums_ref[0] = rhs
        sums_ref[1] = image


def add_gram(gram, pieces, arrays, rows, info_ref, obs):
    me = info_ref[0]
    for (_, pair, offset, length), ref in zip(pieces, arrays):
        slot = lax.broadcasted_iota(jnp.int32, (length, gram.shape[0]), 0)
        slot = slot + (shard_index(me, pair) * rows + offset)
        for t in range(ref.shape[0]):
            tile_rows = ref[t]
            masked = jnp.where(slot < info_ref[1 + obs + t], tile_rows, jnp.zeros_like(tile_rows))
            gram = gram + lax.dot_general(
                masked, tile_rows, (((0,), (0,)), ((), ())), preferred_element_type=F32
            )
    return gram


def keep_kernel(in_ref, out_ref):
    for index in range(in_ref.shape[0]):
        out_ref[index] = in_ref[index]


def twin_kernel(pieces, rows, info_ref, twin_info_ref, alpha_ref, prev_ref, *refs):
    *arrays, part_ref = refs
    users, rank = prev_ref.shape
    obs = alpha_ref.shape[0]
    prev = prev_ref[...]
    gram = add_gram(jnp.zeros((rank, rank), F32), pieces, arrays, rows, info_ref, obs)
    rhs = jnp.zeros((users, rank), F32)
    image = jnp.zeros((users, rank), F32)
    conf = jnp.zeros((users, 1), F32)
    for p in range(obs):
        tile = twin_info_ref[1 + p]
        conf = jnp.maximum(conf, jnp.max(alpha_ref[p], axis=1, keepdims=True))
        for (spot, _, _, length), ref in zip(pieces, arrays):
            items = ref[tile]
            alpha = alpha_ref[p, :, spot : spot + length]
            scores = jnp.dot(prev, items.T, preferred_element_type=F32)
            weights = (alpha * scores).astype(BF16)
            seen = jnp.where(alpha > 0.0, 1.0, 0.0).astype(BF16)
            rhs = rhs + jnp.dot(seen, items, preferred_element_type=F32)
            image = image + jnp.dot(weights, items, preferred_element_type=F32)
    high = gram.astype(BF16)
    low = (gram - high.astype(F32)).astype(BF16)
    image = image + jnp.dot(prev, high, preferred_element_type=F32)
    image = image + jnp.dot(prev, low, preferred_element_type=F32)
    part_ref[...] = (1.0 + conf) * rhs - image


def join_kernel(mine_ref, part_ref, msg_ref):
    pack(mine_ref[...] + part_ref[...], msg_ref)


def collect_kernel(pieces, rows, info_ref, gram_ref, *refs):
    arrays = refs[: len(pieces)]
    picked_ref, turned_ref, high_ref, low_ref = refs[len(pieces) :]
    obs = picked_ref.shape[0]
    for p in range(obs):
        tile = info_ref[1 + p]
        for (spot, _, _, length), ref in zip(pieces, arrays):
            picked_ref[p, spot : spot + length, :] = ref[tile]
        for block in blocks(picked_ref.shape[1]):
            turned_ref[p, :, block] = picked_ref[p, block, :].T
    gram = add_gram(gram_ref[...], pieces, arrays, rows, info_ref, obs)
    high = gram.astype(BF16)
    high_ref[...] = high
    low_ref[...] = (gram - high.astype(F32)).astype(BF16)


def in_order(refs, order):
    return [refs[order.index(bits)] for bits in range(len(order))]


def round_kernel(step_index, order, n_stages, *refs):
    msgs = in_order(refs, order)
    refs = refs[len(order) :]
    prev_ref, high_ref, low_ref = refs[:3]
    alphas, picked, turned = (refs[3 + n * n_stages : 3 + (n + 1) * n_stages] for n in range(3))
    refs = refs[3 + 3 * n_stages :]
    summed = tree_sum([unpack(m) for m in msgs])
    if step_index == 0:
        (r_ref, msg_ref) = refs
        residual = summed - ridge_weight * prev_ref[...].astype(F32)
        direction = residual
        r_ref[...] = residual
    else:
        n_state = 1 if step_index == 1 else 3
        state = refs[:n_state]
        refs = refs[n_state:]
        if step_index == 1:
            residual = direction = state[0][...]
            solution = prev_ref[...].astype(F32)
        else:
            residual, direction, solution = (s[...] for s in state)
        image = summed + ridge_weight * direction
        norm_now = jnp.sum(residual * residual, axis=1, keepdims=True)
        step_size = norm_now / jnp.sum(direction * image, axis=1, keepdims=True)
        solution = solution + step_size * direction
        residual = residual - step_size * image
        norm_next = jnp.sum(residual * residual, axis=1, keepdims=True)
        direction = residual + (norm_next / norm_now) * direction
        if step_index < ITERS - 1:
            r_ref, d_ref, x_ref, msg_ref = refs
            r_ref[...] = residual
        else:
            n_ref, d_ref, x_ref, msg_ref = refs
            n_ref[...] = jnp.broadcast_to(norm_next, n_ref.shape)
        d_ref[...] = direction
        x_ref[...] = solution
    last = step_index == ITERS - 1
    rounded = direction.astype(BF16)
    users = direction.shape[0]
    both = jnp.concatenate([rounded, (direction - rounded.astype(F32)).astype(BF16)], axis=0)
    both = jnp.dot(both, high_ref[...], preferred_element_type=F32)
    image = both[:users] + both[users:] + jnp.dot(rounded, low_ref[...], preferred_element_type=F32)
    if last:
        total = jnp.sum(image * direction, axis=1, keepdims=True)
    for alpha_ref, ref, turned_ref in zip(alphas, picked, turned):
        for p in range(ref.shape[0]):
            for block in blocks(ref.shape[1]):
                items = ref[p, block, :]
                alpha = alpha_ref[p, :, block]
                scores = jnp.dot(rounded, turned_ref[p, :, block], preferred_element_type=F32)
                weights = (alpha * scores).astype(BF16)
                if last:
                    total = total + jnp.sum(weights.astype(F32) * scores, axis=1, keepdims=True)
                else:
                    image = image + jnp.dot(weights, items, preferred_element_type=F32)
    if last:
        msg_ref[...] = row_of(total, msg_ref.shape[0])
    else:
        pack(image, msg_ref)


def final_kernel(order, *refs):
    msgs = in_order(refs, order)
    n_ref, d_ref, x_ref, out_ref = refs[len(order) :]
    direction = d_ref[...]
    total = column_of(tree_sum([m[...] for m in msgs])[:1], 128)
    squares = jnp.sum(direction * direction, axis=1, keepdims=True)
    step_size = n_ref[...] / (total + ridge_weight * squares)
    for at in range(0, direction.shape[1], 128):
        out_ref[:, at : at + 128] = x_ref[:, at : at + 128] + step_size * direction[:, at : at + 128]


def permuted(array, axis, size, target):
    return lax.ppermute(array, axis, [(i, target(i)) for i in range(size)])


def tied(array, token):
    return lax.optimization_barrier((array, token))[0]


def gather_stages(own, size, plan, work, prepare, finish):
    send = functools.partial(permuted, axis="row", size=size)
    held = {0: own}
    bit = 8 if size >= 8 else 1
    while bit < size:
        held.update({s ^ bit: send(a, target=lambda i: i ^ bit) for s, a in held.items()})
        bit *= 2
    rows = own.shape[1]
    if size < 8:
        plan([[((s, s), 0, rows) for s in held]])
        work(list(held.values()))
        return

    def twin(array):
        return send(array, target=lambda i: i ^ 1)

    def first_way(array):
        return send(array, target=lambda i: i ^ (2 + 2 * (i & 1)))

    def second_way(array):
        return send(array, target=lambda i: i ^ (4 - 2 * (i & 1)))

    half = rows // 2
    whole, upper, lower = (0, rows), (0, half), (half, half)
    kinds = [
        [((0, 0), *whole), ((1, 1), *whole)],
        [((2, 4), *whole), ((5, 3), *upper), ((5, 3), *lower), ((4, 2), *whole), ((3, 5), *upper), ((3, 5), *lower)],
        [((6, 6), *whole)],
        [((7, 7), *whole)],
    ]
    early = plan([[((s ^ e, s ^ o), at, n) for s in held for (e, o), at, n in kind] for kind in kinds])

    one = [first_way(a) for a in held.values()]
    two = [second_way(tied(a, early)) for a in held.values()]
    token = work([x for a in held.values() for x in (a, twin(a))])
    ready = prepare(twin)
    one = [tied(a, (token, ready)) for a in one]
    two = [tied(a, token) for a in two]
    far = [second_way(a) for a in one]
    token = work([x for a, b in zip(one, two) for x in (a, twin(a[:, :half]), twin(a[:, half:]), b, twin(b[:, :half]), twin(b[:, half:]))])
    far = [tied(a, token) for a in far]
    finish(far, twin, ready)


def local(mesh, item_factors, tile_counts, observed_tiles, mask_words, confidence, previous):
    n_row, n_col = mesh.shape["row"], mesh.shape["col"]
    tiles, rows, rank = item_factors.shape
    users, obs, width = mask_words.shape
    slots = rows * n_row
    me = lax.axis_index("row").astype(jnp.int32).reshape(1)
    info = jnp.concatenate([me, observed_tiles[0], tile_counts])
    conf = confidence[:, None]
    words = jnp.transpose(mask_words, (1, 0, 2)).astype(BF16)
    shape = jax.ShapeDtypeStruct

    message = shape((users, rank), jnp.int16)
    vec = shape((users, rank), F32)
    sums = shape((2, users, rank), F32)
    gram_shape = shape((rank, rank), F32)
    stages, picked, turned, alphas, carry, scalars = [], [], [], [], [], []

    def masks_of(plan):
        for stage in plan:
            spot, pieces = 0, []
            for pair, offset, length in stage:
                pieces.append((spot, pair, offset, length))
                spot += length
            stages.append(pieces)
        sizes = [sum(length for _, _, _, length in pieces) for pieces in stages]
        *masks, kept_info = (
            call(
                functools.partial(masks_kernel, stages, rows),
                [shape((obs, users, size), F32) for size in sizes],
                (info, words, conf),
                1,
                2 * obs * users * sum(sizes) * width,
                "masks",
                [shape(info.shape, info.dtype)],
            )
        )
        alphas.extend(masks)
        scalars.append(kept_info)
        return alphas

    def work(arrays, closing=False):
        index = len(picked)
        first, last = index == 0, index == len(stages) - 1
        pieces, alpha = stages[index], alphas[index]
        size = alpha.shape[2]
        split = shape((rank, rank), BF16)
        kept, kept_turned, *carried = call(
            functools.partial(gather_kernel, pieces, rows, first, last, closing),
            [shape((obs, size, rank), BF16), shape((obs, rank, size), BF16)]
            + ([split, split, message] if last else [gram_shape, vec if closing else sums]),
            (*scalars, alpha, conf, previous, *arrays, *carry),
            1,
            2 * size * rank * (tiles * rank + 3 * obs * users),
            "stage",
        )
        carry[:] = carried
        picked.append(kept)
        turned.append(kept_turned)
        return carried, alphas

    def prepare(twin):
        (twin_info,) = call(keep_kernel, [], (twin(info),), 1, 0, "keep", [shape(info.shape, info.dtype)])
        return twin_info, twin(alphas[3]), twin(previous)

    def finish(far, twin, ready):
        pieces, alpha = stages[2], alphas[3]
        twin_info, twin_alpha, twin_prev = ready
        size = alpha.shape[2]
        flops = 2 * size * rank * (tiles * rank + 3 * obs * users)
        (part,) = call(
            functools.partial(twin_kernel, pieces, rows),
            [vec],
            (*scalars, twin_info, twin_alpha, twin_prev, *far),
            2,
            flops,
            "twin",
        )
        part = twin(part)
        gram, mine = work(far, True)[0]
        (msg,) = call(join_kernel, [message], (mine, part), 0, 0, "join")
        others = [twin(tied(a, msg)) for a in far]
        kept, kept_turned, high, low = call(
            functools.partial(collect_kernel, stages[3], rows),
            [shape((obs, size, rank), BF16), shape((obs, rank, size), BF16)] + [shape((rank, rank), BF16)] * 2,
            (*scalars, gram, *others),
            1,
            flops,
            "collect",
        )
        picked.append(kept)
        turned.append(kept_turned)
        carry[:] = high, low, msg

    gather_stages(item_factors, n_row, masks_of, work, prepare, finish)
    high, low, msg = carry

    order = [0, *range(2, n_col, 2), *range(1, n_col, 2)]

    def partner(place, bits):
        row, col = place // n_col, place % n_col
        if row & 1 and n_col > 2:
            bits = (bits & ~3) | (0, 2, 1, 3)[bits & 3]
        return row * n_col + (col ^ bits)

    def sent(own, bits):
        return lax.ppermute(own, ("row", "col"), [(i, partner(i, bits)) for i in range(n_row * n_col)])

    def to_all(own, order=order):
        return [own] + [sent(own, bits) for bits in order[1:]]

    state = []
    for index in range(ITERS):
        last = index == ITERS - 1
        msgs = to_all(msg)
        outs = [vec] if index == 0 else [vec, vec, vec]
        if last:
            outs = [shape((users, 128), F32), vec, vec]
        outs.append(shape((8, users), F32) if last else message)
        *state, msg = call(
            functools.partial(round_kernel, index, order, len(picked)),
            outs,
            (*msgs, previous, high, low, *alphas, *picked, *turned, *state),
            0,
            4 * obs * users * slots * rank,
            f"round{index}",
        )
    order = list(range(n_col))
    msgs = to_all(msg, order)
    (out,) = pl.pallas_call(
        functools.partial(final_kernel, order),
        out_shape=[vec],
        in_specs=[VMEM] * (n_col + 3),
        out_specs=[VMEM],
        compiler_params=pltpu.CompilerParams(vmem_limit_bytes=4 * 1024 * 1024),
        name="final",
    )(*msgs, *state)
    return out


def solution(mesh):
    return jax.shard_map(
        functools.partial(local, mesh),
        mesh=mesh,
        in_specs=(
            P("col", "row", None),
            P("col"),
            P("row", "col"),
            P("row", "col", None),
            P("row"),
            P("row", None),
        ),
        out_specs=P("row", None),
        check_vma=False,
    )
```
